256 devices in a mesh: tm: 16 (over x_hi, z), head: 16 (over y, x_lo, core).
Axes of the slice: x: 4 (x_hi: 2, x_lo: 2; x = x_hi * 2 + x_lo), y: 4, z: 8, core: 2. Of those that a mesh axis runs over, the one named last changes fastest.
Arguments:
- tokens: bfloat16 [64, 288, 1408], P('tm'), may hold values from -20 to 20
- norm_gain: float32 [1408], replicated, may hold values from 0.5 to 1.5
- norm_shift: float32 [1408], replicated, may hold values from -3 to 3
- w_qkv: bfloat16 [1408, 16, 264], P(None, 'head'), may hold values from -4 to 4
- output_weight: bfloat16 [1408, 1408], P('head'), may hold values from -0.625 to 0.625
Outputs:
- attended: bfloat16 [64, 288, 1408], P('tm', 'head')
The draws below stay inside these ranges and needn't reach their ends.
All inputs are finite; a program needn't handle non-finite values.
Results may differ from the reference program's by a relative error of at most 0.024.
Values may be sent and summed in bfloat16 or wider, within the bound.
A program may use at most 64 MiB of HBM per device.

```python
import math
import jax
import jax.numpy as jnp
from jax import lax

D = 1408
HEADS = 16
HD = 88
P_SIZE = 288
FRAMES = 64


def draw_tokens(key, part):
    key = jax.random.fold_in(key, 11)
    shape = (FRAMES, P_SIZE, D)
    return jnp.clip(jax.random.normal(key, shape, jnp.float32), -6.0, 6.0).astype(jnp.bfloat16)


def draw_w_qkv(key, part):
    key = jax.random.fold_in(key, 23)
    limit = 6.0 / math.sqrt(D)
    drawn = jax.random.normal(key, (D, HEADS, 3 * HD), jnp.float32) / math.sqrt(D)
    return jnp.clip(drawn, -limit, limit).astype(jnp.bfloat16)


def levels(stream_key, shape, pieces, least, largest):
    loudness = 1.0
    for position, shards_of in pieces:
        heights = jax.random.uniform(jax.random.fold_in(jax.random.fold_in(stream_key, 6), position), (shards_of,), jnp.float32, least / len(pieces), largest / len(pieces))
        loudness = loudness * jnp.repeat(jnp.exp(heights), shape[position] // shards_of).reshape((-1,) + (1,) * (len(shape) - 1 - position))
    return loudness


def scatter_about(key, dims, width, most, shards=(), kind=jnp.bfloat16):
    values = jax.random.normal(key, dims, jnp.float32) * width
    if len(shards) > 0:
        values = levels(key, dims, shards, -0.22, 0.18) * values
    return jnp.clip(values, min=-most, max=most).astype(kind)


def setup_inputs(seed: int = 0) -> dict:
    arg_keys = jax.random.split(jax.random.key(seed), 6)
    tokens = draw_tokens(jax.random.fold_in(arg_keys[5], 71), 0)
    norm_gain = jnp.clip(jax.random.uniform(arg_keys[1], (D,), jnp.float32, 0.5, 1.5), 0.5, 1.5)
    norm_shift = scatter_about(arg_keys[2], (D,), 0.5, 3.0, (), jnp.float32)
    w_qkv = draw_w_qkv(jax.random.fold_in(arg_keys[5], 71), 0)
    output_weight = scatter_about(arg_keys[4], (HEADS * HD, D), HD ** -0.5, 0.625, ((0, 16),))
    return {"tokens": tokens, "norm_gain": norm_gain, "norm_shift": norm_shift, "w_qkv": w_qkv, "output_weight": output_weight}


def layer_norm(row_block, norm_gain, norm_shift):
    values = row_block.astype(jnp.float32)
    row_average = lax.optimization_barrier(jnp.mean(values, axis=-1, keepdims=True))
    centred = values - row_average
    row_var = lax.optimization_barrier(jnp.mean(centred * centred, axis=-1, keepdims=True))
    scaled = centred * lax.rsqrt(row_var + 1e-06) * norm_gain.astype(jnp.float32) + norm_shift.astype(jnp.float32)
    return scaled.astype(jnp.bfloat16)

def one_head(head_block):
    head_size = head_block.shape[-1] // 3
    query_block = head_block[..., :head_size].astype(jnp.float32)
    key_rows = head_block[..., head_size:2 * head_size].astype(jnp.float32)
    value_rows = head_block[..., 2 * head_size:].astype(jnp.float32)
    scores = jnp.einsum('fpd,gpd->pfg', query_block, key_rows) * (1.0 / math.sqrt(head_size))
    row_max = lax.optimization_barrier(jnp.max(scores, axis=-1, keepdims=True))
    exponent = jnp.exp(scores - row_max)
    probs = (exponent / lax.optimization_barrier(jnp.sum(exponent, axis=-1, keepdims=True))).astype(jnp.bfloat16)
    result = jnp.einsum('pfg,gpd->fpd', probs.astype(jnp.float32), value_rows)
    return result.astype(jnp.bfloat16)

def reference(tokens, norm_gain, norm_shift, w_qkv, output_weight):
    normed = layer_norm(tokens, norm_gain, norm_shift)
    packed = jnp.dot(normed.reshape(FRAMES * P_SIZE, D), w_qkv.reshape(D, HEADS * 3 * HD), preferred_element_type=jnp.float32)
    packed = packed.astype(jnp.bfloat16).reshape(FRAMES, P_SIZE, HEADS, 3 * HD)
    per_head = lax.map(one_head, jnp.moveaxis(packed, 2, 0))
    head_outputs = jnp.moveaxis(per_head, 0, 2).reshape(FRAMES * P_SIZE, HEADS * HD)
    attended = jnp.dot(head_outputs, output_weight, preferred_element_type=jnp.float32)
    return attended.astype(jnp.bfloat16).reshape(FRAMES, P_SIZE, D)
```

```python
import math

import jax
import jax.numpy as jnp
from jax import lax
from jax.sharding import PartitionSpec as P


def layer_norm(row_block, norm_gain, norm_shift):
    values = row_block.astype(jnp.float32)
    row_average = jnp.mean(values, axis=-1, keepdims=True)
    centred = values - row_average
    row_var = jnp.mean(centred * centred, axis=-1, keepdims=True)
    scaled = centred * lax.rsqrt(row_var + 1e-06) * norm_gain + norm_shift
    return scaled.astype(jnp.bfloat16)


def project(normed, w_qkv):
    width = normed.shape[-1]
    leading = normed.shape[:-1]
    flat_tokens = jnp.dot(
        normed.reshape(-1, width), w_qkv.reshape(width, -1), preferred_element_type=jnp.float32
    )
    return flat_tokens.astype(jnp.bfloat16).reshape(leading + (w_qkv.shape[2],))


def attend(arrived_slab):
    head_size = arrived_slab.shape[-1] // 3
    query_block = arrived_slab[..., :head_size]
    key_rows = arrived_slab[..., head_size : 2 * head_size]
    value_rows = arrived_slab[..., 2 * head_size :]
    scores = jnp.einsum(
        "fpd,gpd->pfg", query_block, key_rows, preferred_element_type=jnp.float32
    )
    scores = scores * (1.0 / math.sqrt(head_size))
    row_max = jnp.max(scores, axis=-1, keepdims=True)
    exponent = jnp.exp(scores - row_max)
    probs = (exponent / jnp.sum(exponent, axis=-1, keepdims=True)).astype(jnp.bfloat16)
    result = jnp.einsum("pfg,gpd->fpd", probs, value_rows, preferred_element_type=jnp.float32)
    return result.astype(jnp.bfloat16)


def on_device(tokens, norm_gain, norm_shift, w_qkv, output_weight):
    whole_weight = lax.all_gather(output_weight, "head", axis=0, tiled=True)
    packed = project(layer_norm(tokens, norm_gain, norm_shift), w_qkv)
    arrived = lax.all_to_all(packed, "tm", split_axis=1, concat_axis=0, tiled=True)
    head_outputs = attend(arrived)
    own_frames = lax.all_to_all(head_outputs, "tm", split_axis=0, concat_axis=1, tiled=True)
    own_rows = lax.all_to_all(own_frames, "head", split_axis=1, concat_axis=2, tiled=True)
    return jnp.einsum(
        "fpz,ze->fpe", own_rows, whole_weight, preferred_element_type=jnp.float32
    ).astype(jnp.bfloat16)


def solution(mesh):
    return jax.shard_map(
        on_device,
        mesh=mesh,
        in_specs=(P("tm", None, None), P(), P(), P(None, "head", None), P("head", None)),
        out_specs=P("tm", "head", None),
        check_vma=False,
    )
```

```python
import math

import jax
import jax.numpy as jnp
from jax import lax
from jax.experimental import pallas as pl
from jax.experimental.pallas import tpu as pltpu
from jax.sharding import PartitionSpec as P

MESH = pl.DeviceIdType.MESH
D = 1408
HD = 88
FR = 4
PATCHES = 288
NT = 16
NH = 16
NZ = 8
HALF = PATCHES // 2
BLOCKS = 8
QA, QB = 5, 4
TA, TB = 2 * QA + 1, 2 * QB + 1
WROWS = 96
F32 = jnp.float32
BF16 = jnp.bfloat16


def kernel(
    tok_hbm, gain, shift, wq, wo, out,
    tok, wperm, packed, send_a, send_b, recv, ret_send, ret_recv, wbuf,
    tok_sem, p1_send, p1_recv, rt_send, rt_recv_a, rt_recv_b, loc_sem, w_send, w_recv,
):
    t = lax.axis_index("tm")
    h = lax.axis_index("head")
    xh, z = t // NZ, t % NZ
    chip, core = h // 2, h % 2
    y, xl = chip // 2, chip % 2
    is_a = xh == core

    tok_copies = [
        pltpu.make_async_copy(
            tok_hbm.at[:, pl.ds(k * HALF, HALF), :], tok.at[:, pl.ds(k * HALF, HALF), :], tok_sem.at[k]
        )
        for k in range(2)
    ]
    for copy in tok_copies:
        copy.start()

    def head_of(y_, xl_, core_):
        return ((y_ + 4) % 4) * 4 + xl_ * 2 + core_

    x_cross = ((1 - xh) * NZ + z, head_of(y, 1 - xl, core))
    barrier = pltpu.get_barrier_semaphore()

    @pl.loop(1, NT)
    def _(k):
        pl.semaphore_signal(barrier, inc=1, device_id=((t + k) % NT, h), device_id_type=MESH)
        pl.semaphore_signal(barrier, inc=1, device_id=(t, (h + k) % NH), device_id_type=MESH)

    pl.semaphore_signal(barrier, inc=1, device_id=x_cross, device_id_type=MESH)

    w = wq[...].astype(F32)
    wperm[:, 0:128] = jnp.concatenate([w[:, 0:88], w[:, 176:216]], axis=1).astype(BF16)
    wperm[:, 128:256] = jnp.concatenate([w[:, 88:176], w[:, 216:256]], axis=1).astype(BF16)
    wperm[:, 256:384] = jnp.concatenate(
        [w[:, 256:264], jnp.zeros((D, 120), F32)], axis=1
    ).astype(BF16)
    wbuf[h, pl.ds(0, WROWS), :] = jnp.concatenate(
        [wo[...].astype(F32), jnp.zeros((WROWS - HD, D), F32)], axis=0
    ).astype(BF16)

    @pl.loop(0, NH)
    def _(k):
        wbuf[k, pl.ds(WROWS, 128 - WROWS), :] = jnp.zeros((128 - WROWS, D), BF16)

    def project(k):
        tok_copies[k].wait()

        @pl.loop(0, FR)
        def _(f):
            values = tok[f, pl.ds(k * HALF, HALF), :].astype(F32)
            average = jnp.mean(values, axis=-1, keepdims=True)
            centred = values - average
            var = jnp.mean(centred * centred, axis=-1, keepdims=True)
            normed = centred * lax.rsqrt(var + 1e-06) * gain[...] + shift[...]
            packed[f] = jnp.dot(normed.astype(BF16), wperm[...], preferred_element_type=F32)

        parts = [packed[f].reshape(HALF // 8, 8, 384) for f in range(FR)]
        low = lax.broadcasted_iota(jnp.int32, parts[0].shape, 1) < 4
        turned = [pltpu.roll(part, 4, 1) for part in parts]
        even = jnp.concatenate(
            [jnp.where(low, parts[0], turned[1]), jnp.where(low, parts[2], turned[3])], axis=1
        )
        odd = jnp.concatenate(
            [jnp.where(low, turned[0], parts[1]), jnp.where(low, turned[2], parts[3])], axis=1
        )
        for b in range(BLOCKS // 2):
            for buf, first, count in ((send_a, 0, QA), (send_b, QA, QB)):
                rest = None
                for j in range(count):
                    q = 9 * b + first + j
                    tile = (odd if q % 2 else even)[q // 2]
                    at = k * (BLOCKS // 2) + b
                    buf[at, 1 + 2 * j] = tile[:, 0:128].astype(BF16)
                    buf[at, 2 + 2 * j] = tile[:, 128:256].astype(BF16)
                    left = tile[:, 256:384]
                    if j:
                        left = pltpu.roll(left, 8 * j, 1)
                    rest = left if rest is None else rest + left
                buf[at, 0] = rest.astype(BF16)

    def p1_copy(b, kind):
        buf, tiles = (send_a, TA) if kind == 0 else (send_b, TB)
        to_t = (core if kind == 0 else 1 - core) * NZ + (b + chip) % NZ
        src, dst = buf.at[b], recv.at[t, pl.ds(0, tiles)]
        remote = pltpu.make_async_remote_copy(
            src_ref=src, dst_ref=dst, send_sem=p1_send.at[2 * b + kind], recv_sem=p1_recv.at[t],
            device_id=(to_t, h), device_id_type=MESH,
        )
        return to_t == t, remote, pltpu.make_async_copy(src, dst, loc_sem.at[0])

    def p1_start(b, kind):
        own, remote, local = p1_copy(b, kind)

        @pl.when(own)
        def _():
            local.start()

        @pl.when(jnp.logical_not(own))
        def _():
            remote.start()

    def start_blocks(k):
        @pl.loop(0, BLOCKS // 2)
        def _(n):
            p1_start(k * (BLOCKS // 2) + n, 0)
            p1_start(k * (BLOCKS // 2) + n, 1)

    sib = (t, chip * 2 + 1 - core)
    x_near = (t, head_of(y, 1 - xl, core))
    y_up, y_down = (t, head_of(y + 1, xl, core)), (t, head_of(y - 1, xl, core))
    slot_x = head_of(y, 1 - xl, core)
    FULL, LOW, HIGH = (0, WROWS), (0, WROWS // 2), (WROWS // 2, WROWS // 2)

    def w_copy(slot, rows, to, n_send, n_recv):
        ref = wbuf.at[slot, pl.ds(rows[0], rows[1]), :]
        return pltpu.make_async_remote_copy(
            src_ref=ref, dst_ref=ref, send_sem=w_send.at[n_send], recv_sem=w_recv.at[n_recv],
            device_id=to, device_id_type=MESH,
        )

    def slot(dy, other_x, other_core):
        return head_of(y + dy, (1 - xl) if other_x else xl, (1 - core) if other_core else core)

    w_sends = []

    def w_start(copy):
        copy.start()
        w_sends.append(copy)

    def w_wait(slot_, rows, n_recv):
        w_copy(slot_, rows, sib, 0, n_recv).wait_recv()

    def w_first():
        w_start(w_copy(h, LOW, x_near, 0, 8))
        w_start(w_copy(h, HIGH, x_cross, 1, 9))
        w_start(w_copy(h, FULL, y_up, 2, 10))
        w_start(w_copy(h, FULL, y_down, 3, 11))
        w_start(w_copy(h, FULL, sib, 4, 0))

    def w_second():
        w_wait(slot_x, LOW, 8)
        w_wait(slot_x, HIGH, 9)
        w_start(w_copy(slot_x, FULL, y_up, 5, 12))
        w_start(w_copy(slot_x, FULL, y_down, 6, 13))
        w_start(w_copy(slot_x, FULL, sib, 7, 1))

    def w_third():
        for n, (dy, other_x, rows, to) in enumerate(
            ((-1, 0, LOW, y_up), (1, 0, HIGH, y_down), (-1, 1, LOW, y_up), (1, 1, HIGH, y_down))
        ):
            at = slot(dy, other_x, 0)
            w_wait(at, FULL, 10 + n)
            w_start(w_copy(at, rows, to, 8 + n, 14 + n))
            w_start(w_copy(at, FULL, sib, 12 + n, 2 + n))

    def w_fourth():
        for other_x in (0, 1):
            at = slot(2, other_x, 0)
            w_wait(at, LOW, 14 + 2 * other_x)
            w_wait(at, HIGH, 15 + 2 * other_x)
            w_start(w_copy(at, FULL, sib, 16 + other_x, 6 + other_x))

    def w_last():
        for n, (dy, other_x) in enumerate(
            ((0, 0), (0, 1), (-1, 0), (1, 0), (-1, 1), (1, 1), (2, 0), (2, 1))
        ):
            w_wait(slot(dy, other_x, 1), FULL, n)

    project(0)
    pl.semaphore_wait(barrier, 2 * (NT - 1) + 1)
    start_blocks(0)
    w_first()
    project(1)
    start_blocks(1)
    w_second()
    w_third()

    def p1_wait(tiles):
        @pl.loop(0, NT)
        def _(s):
            ref = recv.at[s, pl.ds(0, tiles)]

            @pl.when(s == t)
            def _():
                pltpu.make_async_copy(ref, ref, loc_sem.at[0]).wait()

            @pl.when(s != t)
            def _():
                pltpu.make_async_remote_copy(
                    src_ref=ref, dst_ref=ref, send_sem=p1_send.at[0], recv_sem=p1_recv.at[s],
                    device_id=(s, h), device_id_type=MESH,
                ).wait_recv()

    @pl.when(is_a)
    def _():
        p1_wait(TA)

    @pl.when(jnp.logical_not(is_a))
    def _():
        p1_wait(TB)

    rows = 16 * NT
    lane = lax.broadcasted_iota(jnp.int32, (rows, 128), 1)
    same = (
        lax.broadcasted_iota(jnp.int32, (rows, rows), 0) % 4
        == lax.broadcasted_iota(jnp.int32, (rows, rows), 1) % 4
    )

    def attend(j):
        first = recv[:, 1 + 2 * j].reshape(rows, 128)
        second = recv[:, 2 + 2 * j].reshape(rows, 128)
        rest = recv[:, 0].reshape(rows, 128)
        scores = lax.dot_general(
            first[:, :HD], second[:, :HD], (((1,), (1,)), ((), ())), preferred_element_type=F32
        ) * (1.0 / math.sqrt(HD))
        scores = jnp.where(same, scores, -jnp.inf)
        exponent = jnp.exp(scores - jnp.max(scores, axis=-1, keepdims=True))
        probs = (exponent / jnp.sum(exponent, axis=-1, keepdims=True)).astype(BF16)
        values = jnp.concatenate([first, second, rest], axis=1)
        mixed = jnp.dot(probs, values, preferred_element_type=F32)
        head = jnp.where(
            lane < 40,
            pltpu.roll(mixed[:, 0:128], 40, 1),
            jnp.where(
                lane < 80,
                pltpu.roll(mixed[:, 128:256], 80, 1),
                jnp.where(lane < HD, pltpu.roll(mixed[:, 256:384], 80 - 8 * j, 1), 0.0),
            ),
        )
        ret_send[:, j] = head.astype(BF16).reshape(NT, 16, 128)

    for j in range(QB):
        attend(j)

    @pl.when(is_a)
    def _():
        attend(QA - 1)

    to_chip = (z - chip + NZ) % NZ

    def ret_copy(to_t, to_core, src, dst, n_send, sem):
        to_h = to_chip * 2 + to_core
        own = jnp.logical_and(to_t == t, to_h == h)
        remote = pltpu.make_async_remote_copy(
            src_ref=src, dst_ref=dst, send_sem=rt_send.at[n_send], recv_sem=sem,
            device_id=(to_t, to_h), device_id_type=MESH,
        )
        return own, remote, pltpu.make_async_copy(src, dst, loc_sem.at[1])

    def ret_whole(to_t):
        return ret_copy(to_t, 0, ret_send.at[to_t], ret_recv.at[h], to_t, rt_recv_a.at[h])

    def ret_shared(to_t):
        return ret_copy(
            to_t, 1, ret_send.at[to_t, pl.ds(QB, 1)], ret_recv.at[h, pl.ds(0, 1)],
            NT + to_t, rt_recv_a.at[h],
        )

    def ret_rest(to_t):
        return ret_copy(
            to_t, 1, ret_send.at[to_t, pl.ds(0, QB)], ret_recv.at[h, pl.ds(1, QB)],
            to_t, rt_recv_b.at[h],
        )

    def start(triple):
        own, remote, local = triple

        @pl.when(own)
        def _():
            local.start()

        @pl.when(jnp.logical_not(own))
        def _():
            remote.start()

    def finish(triple):
        own, remote, _ = triple

        @pl.when(jnp.logical_not(own))
        def _():
            remote.wait_send()

    @pl.when(is_a)
    def _():
        @pl.loop(0, NT)
        def _(k):
            to_t = (t + k) % NT
            start(ret_whole(to_t))
            start(ret_shared(to_t))

    @pl.when(jnp.logical_not(is_a))
    def _():
        @pl.loop(0, NT)
        def _(k):
            start(ret_rest((t + k) % NT))

    w_fourth()
    w_last()

    def ret_wait(ref, from_t, from_h, sem):
        own = jnp.logical_and(from_t == t, from_h == h)

        @pl.when(own)
        def _():
            pltpu.make_async_copy(ref, ref, loc_sem.at[1]).wait()

        @pl.when(jnp.logical_not(own))
        def _():
            pltpu.make_async_remote_copy(
                src_ref=ref, dst_ref=ref, send_sem=rt_send.at[0], recv_sem=sem,
                device_id=(from_t, from_h), device_id_type=MESH,
            ).wait_recv()

    @pl.loop(0, NH)
    def _(g):
        from_z = (chip + g // 2) % NZ
        t_a = (g % 2) * NZ + from_z
        t_b = (1 - g % 2) * NZ + from_z

        @pl.when(core == 0)
        def _():
            ret_wait(ret_recv.at[g], t_a, g, rt_recv_a.at[g])

        @pl.when(core == 1)
        def _():
            ret_wait(ret_recv.at[g, pl.ds(0, 1)], t_a, g, rt_recv_a.at[g])
            ret_wait(ret_recv.at[g, pl.ds(1, QB)], t_b, g, rt_recv_b.at[g])

    left = jnp.concatenate([ret_recv[g].reshape(16 * QA, 128) for g in range(NH)], axis=1)
    total = jnp.dot(left, wbuf[...].reshape(NH * 128, D), preferred_element_type=F32)

    parts = total.reshape(2 * QA, 8, D)
    low = lax.broadcasted_iota(jnp.int32, (8, D), 0) < 4
    for f in range(FR):
        for pair in range(3):
            lo = parts[4 * pair + f // 2]
            hi = parts[4 * pair + 2 + f // 2] if pair < 2 else lo
            if f % 2 == 0:
                rows_ = jnp.where(low, lo, pltpu.roll(hi, 4, 0))
            else:
                rows_ = jnp.where(low, pltpu.roll(lo, 4, 0), hi)
            out[f, pl.ds(8 * pair, 8), :] = rows_

    @pl.loop(0, BLOCKS)
    def _(b):
        for kind in range(2):
            finish(p1_copy(b, kind))

    @pl.when(is_a)
    def _():
        @pl.loop(0, NT)
        def _(to_t):
            finish(ret_whole(to_t))
            finish(ret_shared(to_t))

    @pl.when(jnp.logical_not(is_a))
    def _():
        @pl.loop(0, NT)
        def _(to_t):
            finish(ret_rest(to_t))

    for copy in w_sends:
        copy.wait_send()


def on_device(tokens, norm_gain, norm_shift, w_qkv, output_weight):
    vmem = pl.BlockSpec(memory_space=pltpu.VMEM)
    dma = pltpu.SemaphoreType.DMA
    rows = pl.pallas_call(
        kernel,
        out_shape=jax.ShapeDtypeStruct((FR, 24, D), F32),
        in_specs=[pl.BlockSpec(memory_space=pl.ANY), vmem, vmem, vmem, vmem],
        out_specs=vmem,
        scratch_shapes=[
            pltpu.VMEM((FR, PATCHES, D), BF16),
            pltpu.VMEM((D, 384), BF16),
            pltpu.VMEM((FR, HALF, 384), F32),
            pltpu.VMEM((BLOCKS, TA, 16, 128), BF16),
            pltpu.VMEM((BLOCKS, TB, 16, 128), BF16),
            pltpu.VMEM((NT, TA, 16, 128), BF16),
            pltpu.VMEM((NT, QA, 16, 128), BF16),
            pltpu.VMEM((NH, QA, 16, 128), BF16),
            pltpu.VMEM((NH, 128, D), BF16),
            dma((2,)),
            dma((2 * BLOCKS,)),
            dma((NT,)),
            dma((2 * NT,)),
            dma((NH,)),
            dma((NH,)),
            dma((2,)),
            dma((18,)),
            dma((18,)),
        ],
        compiler_params=pltpu.CompilerParams(
            collective_id=0, has_side_effects=True, vmem_limit_bytes=48 * 1024 * 1024
        ),
        cost_estimate=pl.CostEstimate(
            flops=2 * FR * PATCHES * D * 264 + 2 * 72 * D * D,
            bytes_accessed=5_000_000,
            transcendentals=18 * 64 * 64,
        ),
    )(
        tokens,
        norm_gain.reshape(1, D),
        norm_shift.reshape(1, D),
        w_qkv.reshape(D, 3 * HD),
        output_weight,
    )
    core = lax.axis_index("head") % 2
    return lax.dynamic_slice_in_dim(rows, 2 * core, 18, axis=1).astype(BF16)


def solution(mesh):
    return jax.shard_map(
        on_device,
        mesh=mesh,
        in_specs=(P("tm", None, None), P(), P(), P(None, "head", None), P("head", None)),
        out_specs=P("tm", "head", None),
        check_vma=False,
    )
```

```python
import math

import jax
import jax.numpy as jnp
from jax import lax
from jax.experimental import pallas as pl
from jax.experimental.pallas import tpu as pltpu
from jax.sharding import PartitionSpec as P

MESH = pl.DeviceIdType.MESH
D = 1408
HD = 88
FR = 4
PATCHES = 288
NT = 16
NH = 16
NZ = 8
HALF = PATCHES // 2
BLOCKS = 8
QA, QB = 5, 4
TA, TB = 2 * QA + 1, 2 * QB + 1
WROWS = 96
F32 = jnp.float32
BF16 = jnp.bfloat16


def kernel(
    tok_hbm, gain_row, shift_row, wq_hbm, wo_hbm, out,
    tok, wq, wo, wperm, packed, send_a, send_b, recv, ret_send, ret_recv, wbuf,
    tok_sem, in_sem, p1_send, p1_recv, rt_send, rt_recv_a, rt_recv_b, loc_sem, w_send, w_recv,
):
    t = lax.axis_index("tm")
    h = lax.axis_index("head")
    xh, z = t // NZ, t % NZ
    chip, core = h // 2, h % 2
    y, xl = chip // 2, chip % 2
    is_a = xh == core

    tok_copies = [
        pltpu.make_async_copy(
            tok_hbm.at[:, pl.ds(k * HALF, HALF), :], tok.at[:, pl.ds(k * HALF, HALF), :], tok_sem.at[k]
        )
        for k in range(2)
    ]
    wq_copy = pltpu.make_async_copy(wq_hbm, wq, in_sem.at[0])
    wo_copy = pltpu.make_async_copy(wo_hbm, wo, in_sem.at[1])
    tok_copies[0].start()
    wq_copy.start()
    tok_copies[1].start()
    wo_copy.start()

    def head_of(y_, xl_, core_):
        return ((y_ + 4) % 4) * 4 + xl_ * 2 + core_

    x_cross = ((1 - xh) * NZ + z, head_of(y, 1 - xl, core))
    barrier = pltpu.get_barrier_semaphore()

    @pl.loop(1, NT)
    def _(k):
        pl.semaphore_signal(barrier, inc=1, device_id=((t + k) % NT, h), device_id_type=MESH)
        pl.semaphore_signal(barrier, inc=1, device_id=(t, (h + k) % NH), device_id_type=MESH)

    pl.semaphore_signal(barrier, inc=1, device_id=x_cross, device_id_type=MESH)

    wq_copy.wait()
    w = wq[...].astype(F32)
    wperm[...] = jnp.concatenate(
        [w[0:88], w[176:216], w[88:176], w[216:264], jnp.zeros((120, D), F32)], axis=0
    ).astype(BF16)
    wo_copy.wait()
    wbuf[h, pl.ds(0, WROWS), :] = jnp.concatenate(
        [wo[...].astype(F32), jnp.zeros((WROWS - HD, D), F32)], axis=0
    ).astype(BF16)

    @pl.loop(0, NH)
    def _(k):
        wbuf[k, pl.ds(WROWS, 128 - WROWS), :] = jnp.zeros((128 - WROWS, D), BF16)

    gain = gain_row[...].reshape(1, D)
    shift = shift_row[...].reshape(1, D)

    def project(k):
        tok_copies[k].wait()

        @pl.loop(0, FR)
        def _(f):
            values = tok[f, pl.ds(k * HALF, HALF), :].astype(F32)
            average = jnp.mean(values, axis=-1, keepdims=True)
            centred = values - average
            var = jnp.mean(centred * centred, axis=-1, keepdims=True)
            normed = centred * lax.rsqrt(var + 1e-06) * gain + shift
            packed[f] = lax.dot_general(
                normed.astype(BF16), wperm[...], (((1,), (1,)), ((), ())), preferred_element_type=F32
            )

        parts = [packed[f].reshape(HALF // 8, 8, 384) for f in range(FR)]
        low = lax.broadcasted_iota(jnp.int32, parts[0].shape, 1) < 4
        turned = [pltpu.roll(part, 4, 1) for part in parts]
        even = jnp.concatenate(
            [jnp.where(low, parts[0], turned[1]), jnp.where(low, parts[2], turned[3])], axis=1
        )
        odd = jnp.concatenate(
            [jnp.where(low, turned[0], parts[1]), jnp.where(low, turned[2], parts[3])], axis=1
        )
        for b in range(BLOCKS // 2):
            for buf, first, count in ((send_a, 0, QA), (send_b, QA, QB)):
                rest = None
                for j in range(count):
                    q = 9 * b + first + j
                    tile = (odd if q % 2 else even)[q // 2]
                    at = k * (BLOCKS // 2) + b
                    buf[at, 1 + 2 * j] = tile[:, 0:128].astype(BF16)
                    buf[at, 2 + 2 * j] = tile[:, 128:256].astype(BF16)
                    left = tile[:, 256:384]
                    if j:
                        left = pltpu.roll(left, 8 * j, 1)
                    rest = left if rest is None else rest + left
                buf[at, 0] = rest.astype(BF16)

    def p1_copy(b, kind):
        buf, tiles = (send_a, TA) if kind == 0 else (send_b, TB)
        to_t = (core if kind == 0 else 1 - core) * NZ + (b + chip) % NZ
        src, dst = buf.at[b], recv.at[t, pl.ds(0, tiles)]
        remote = pltpu.make_async_remote_copy(
            src_ref=src, dst_ref=dst, send_sem=p1_send.at[2 * b + kind], recv_sem=p1_recv.at[t],
            device_id=(to_t, h), device_id_type=MESH,
        )
        return to_t == t, remote, pltpu.make_async_copy(src, dst, loc_sem.at[0])

    def p1_start(b, kind):
        own, remote, local = p1_copy(b, kind)

        @pl.when(own)
        def _():
            local.start()

        @pl.when(jnp.logical_not(own))
        def _():
            remote.start()

    def start_blocks(k):
        @pl.loop(0, BLOCKS // 2)
        def _(n):
            p1_start(k * (BLOCKS // 2) + n, 0)
            p1_start(k * (BLOCKS // 2) + n, 1)

    sib = (t, chip * 2 + 1 - core)
    x_near = (t, head_of(y, 1 - xl, core))
    y_up, y_down = (t, head_of(y + 1, xl, core)), (t, head_of(y - 1, xl, core))
    slot_x = head_of(y, 1 - xl, core)
    FULL, LOW, HIGH = (0, WROWS), (0, WROWS // 2), (WROWS // 2, WROWS // 2)

    def w_copy(slot, rows, to, n_send, n_recv):
        ref = wbuf.at[slot, pl.ds(rows[0], rows[1]), :]
        return pltpu.make_async_remote_copy(
            src_ref=ref, dst_ref=ref, send_sem=w_send.at[n_send], recv_sem=w_recv.at[n_recv],
            device_id=to, device_id_type=MESH,
        )

    def slot(dy, other_x, other_core):
        return head_of(y + dy, (1 - xl) if other_x else xl, (1 - core) if other_core else core)

    w_sends = []

    def w_start(copy):
        copy.start()
        w_sends.append(copy)

    def w_wait(slot_, rows, n_recv):
        w_copy(slot_, rows, sib, 0, n_recv).wait_recv()

    def w_first():
        w_start(w_copy(h, LOW, x_near, 0, 8))
        w_start(w_copy(h, HIGH, x_cross, 1, 9))
        w_start(w_copy(h, FULL, y_up, 2, 10))
        w_start(w_copy(h, FULL, y_down, 3, 11))
        w_start(w_copy(h, FULL, sib, 4, 0))

    def w_second():
        w_wait(slot_x, LOW, 8)
        w_wait(slot_x, HIGH, 9)
        w_start(w_copy(slot_x, FULL, y_up, 5, 12))
        w_start(w_copy(slot_x, FULL, y_down, 6, 13))
        w_start(w_copy(slot_x, FULL, sib, 7, 1))

    def w_third():
        for n, (dy, other_x, rows, to) in enumerate(
            ((-1, 0, LOW, y_up), (1, 0, HIGH, y_down), (-1, 1, LOW, y_up), (1, 1, HIGH, y_down))
        ):
            at = slot(dy, other_x, 0)
            w_wait(at, FULL, 10 + n)
            w_start(w_copy(at, rows, to, 8 + n, 14 + n))
            w_start(w_copy(at, FULL, sib, 12 + n, 2 + n))

    def w_fourth():
        for other_x in (0, 1):
            at = slot(2, other_x, 0)
            w_wait(at, LOW, 14 + 2 * other_x)
            w_wait(at, HIGH, 15 + 2 * other_x)
            w_start(w_copy(at, FULL, sib, 16 + other_x, 6 + other_x))

    def w_last():
        for n, (dy, other_x) in enumerate(
            ((0, 0), (0, 1), (-1, 0), (1, 0), (-1, 1), (1, 1), (2, 0), (2, 1))
        ):
            w_wait(slot(dy, other_x, 1), FULL, n)

    project(0)
    pl.semaphore_wait(barrier, 2 * (NT - 1) + 1)
    start_blocks(0)
    w_first()
    project(1)
    start_blocks(1)
    w_second()
    w_third()

    def p1_wait(tiles):
        @pl.loop(0, NT)
        def _(s):
            ref = recv.at[s, pl.ds(0, tiles)]

            @pl.when(s == t)
            def _():
                pltpu.make_async_copy(ref, ref, loc_sem.at[0]).wait()

            @pl.when(s != t)
            def _():
                pltpu.make_async_remote_copy(
                    src_ref=ref, dst_ref=ref, send_sem=p1_send.at[0], recv_sem=p1_recv.at[s],
                    device_id=(s, h), device_id_type=MESH,
                ).wait_recv()

    @pl.when(is_a)
    def _():
        p1_wait(TA)

    @pl.when(jnp.logical_not(is_a))
    def _():
        p1_wait(TB)

    rows = 16 * NT
    lane = lax.broadcasted_iota(jnp.int32, (rows, 128), 1)
    same = (
        lax.broadcasted_iota(jnp.int32, (rows, rows), 0) % 4
        == lax.broadcasted_iota(jnp.int32, (rows, rows), 1) % 4
    )

    def attend(j):
        first = recv[:, 1 + 2 * j].reshape(rows, 128)
        second = recv[:, 2 + 2 * j].reshape(rows, 128)
        rest = recv[:, 0].reshape(rows, 128)
        scores = lax.dot_general(
            first[:, :HD], second[:, :HD], (((1,), (1,)), ((), ())), preferred_element_type=F32
        ) * (1.0 / math.sqrt(HD))
        scores = jnp.where(same, scores, -jnp.inf)
        exponent = jnp.exp(scores - jnp.max(scores, axis=-1, keepdims=True))
        probs = (exponent / jnp.sum(exponent, axis=-1, keepdims=True)).astype(BF16)
        values = jnp.concatenate([first, second, rest], axis=1)
        mixed = jnp.dot(probs, values, preferred_element_type=F32)
        head = jnp.where(
            lane < 40,
            pltpu.roll(mixed[:, 0:128], 40, 1),
            jnp.where(
                lane < 80,
                pltpu.roll(mixed[:, 128:256], 80, 1),
                jnp.where(lane < HD, pltpu.roll(mixed[:, 256:384], 80 - 8 * j, 1), 0.0),
            ),
        )
        ret_send[:, j] = head.astype(BF16).reshape(NT, 16, 128)

    for j in range(QB):
        attend(j)

    @pl.when(is_a)
    def _():
        attend(QA - 1)

    to_chip = (z - chip + NZ) % NZ

    def ret_copy(to_t, to_core, src, dst, n_send, sem):
        to_h = to_chip * 2 + to_core
        own = jnp.logical_and(to_t == t, to_h == h)
        remote = pltpu.make_async_remote_copy(
            src_ref=src, dst_ref=dst, send_sem=rt_send.at[n_send], recv_sem=sem,
            device_id=(to_t, to_h), device_id_type=MESH,
        )
        return own, remote, pltpu.make_async_copy(src, dst, loc_sem.at[1])

    def ret_whole(to_t):
        return ret_copy(to_t, 0, ret_send.at[to_t], ret_recv.at[h], to_t, rt_recv_a.at[h])

    def ret_shared(to_t):
        return ret_copy(
            to_t, 1, ret_send.at[to_t, pl.ds(QB, 1)], ret_recv.at[h, pl.ds(0, 1)],
            NT + to_t, rt_recv_a.at[h],
        )

    def ret_rest(to_t):
        return ret_copy(
            to_t, 1, ret_send.at[to_t, pl.ds(0, QB)], ret_recv.at[h, pl.ds(1, QB)],
            to_t, rt_recv_b.at[h],
        )

    def start(triple):
        own, remote, local = triple

        @pl.when(own)
        def _():
            local.start()

        @pl.when(jnp.logical_not(own))
        def _():
            remote.start()

    def finish(triple):
        own, remote, _ = triple

        @pl.when(jnp.logical_not(own))
        def _():
            remote.wait_send()

    @pl.when(is_a)
    def _():
        @pl.loop(0, NT)
        def _(k):
            to_t = (t + k) % NT
            start(ret_whole(to_t))
            start(ret_shared(to_t))

    @pl.when(jnp.logical_not(is_a))
    def _():
        @pl.loop(0, NT)
        def _(k):
            start(ret_rest((t + k) % NT))

    w_fourth()
    w_last()

    def ret_wait(ref, from_t, from_h, sem):
        own = jnp.logical_and(from_t == t, from_h == h)

        @pl.when(own)
        def _():
            pltpu.make_async_copy(ref, ref, loc_sem.at[1]).wait()

        @pl.when(jnp.logical_not(own))
        def _():
            pltpu.make_async_remote_copy(
                src_ref=ref, dst_ref=ref, send_sem=rt_send.at[0], recv_sem=sem,
                device_id=(from_t, from_h), device_id_type=MESH,
            ).wait_recv()

    @pl.loop(0, NH)
    def _(g):
        from_z = (chip + g // 2) % NZ
        t_a = (g % 2) * NZ + from_z
        t_b = (1 - g % 2) * NZ + from_z

        @pl.when(core == 0)
        def _():
            ret_wait(ret_recv.at[g], t_a, g, rt_recv_a.at[g])

        @pl.when(core == 1)
        def _():
            ret_wait(ret_recv.at[g, pl.ds(0, 1)], t_a, g, rt_recv_a.at[g])
            ret_wait(ret_recv.at[g, pl.ds(1, QB)], t_b, g, rt_recv_b.at[g])

    left = jnp.concatenate([ret_recv[g].reshape(16 * QA, 128) for g in range(NH)], axis=1)
    total = jnp.dot(left, wbuf[...].reshape(NH * 128, D), preferred_element_type=F32)

    parts = total.reshape(2 * QA, 8, D)
    low = lax.broadcasted_iota(jnp.int32, (8, D), 0) < 4
    for f in range(FR):
        for pair in range(3):
            lo = parts[4 * pair + f // 2]
            hi = parts[4 * pair + 2 + f // 2] if pair < 2 else lo
            if f % 2 == 0:
                rows_ = jnp.where(low, lo, pltpu.roll(hi, 4, 0))
            else:
                rows_ = jnp.where(low, pltpu.roll(lo, 4, 0), hi)
            out[f, pl.ds(8 * pair, 8), :] = rows_

    @pl.loop(0, BLOCKS)
    def _(b):
        for kind in range(2):
            finish(p1_copy(b, kind))

    @pl.when(is_a)
    def _():
        @pl.loop(0, NT)
        def _(to_t):
            finish(ret_whole(to_t))
            finish(ret_shared(to_t))

    @pl.when(jnp.logical_not(is_a))
    def _():
        @pl.loop(0, NT)
        def _(to_t):
            finish(ret_rest(to_t))

    for copy in w_sends:
        copy.wait_send()


def on_device(tokens, norm_gain, norm_shift, w_qkv, output_weight):
    vmem = pl.BlockSpec(memory_space=pltpu.VMEM)
    hbm = pl.BlockSpec(memory_space=pl.ANY)
    dma = pltpu.SemaphoreType.DMA
    rows = pl.pallas_call(
        kernel,
        out_shape=jax.ShapeDtypeStruct((FR, 24, D), F32),
        in_specs=[hbm, vmem, vmem, hbm, hbm],
        out_specs=vmem,
        scratch_shapes=[
            pltpu.VMEM((FR, PATCHES, D), BF16),
            pltpu.VMEM((3 * HD, D), BF16),
            pltpu.VMEM((HD, D), BF16),
            pltpu.VMEM((384, D), BF16),
            pltpu.VMEM((FR, HALF, 384), F32),
            pltpu.VMEM((BLOCKS, TA, 16, 128), BF16),
            pltpu.VMEM((BLOCKS, TB, 16, 128), BF16),
            pltpu.VMEM((NT, TA, 16, 128), BF16),
            pltpu.VMEM((NT, QA, 16, 128), BF16),
            pltpu.VMEM((NH, QA, 16, 128), BF16),
            pltpu.VMEM((NH, 128, D), BF16),
            dma((2,)),
            dma((2,)),
            dma((2 * BLOCKS,)),
            dma((NT,)),
            dma((2 * NT,)),
            dma((NH,)),
            dma((NH,)),
            dma((2,)),
            dma((18,)),
            dma((18,)),
        ],
        compiler_params=pltpu.CompilerParams(
            collective_id=0, has_side_effects=True, vmem_limit_bytes=60 * 1024 * 1024
        ),
        cost_estimate=pl.CostEstimate(
            flops=2 * FR * PATCHES * D * 264 + 2 * 72 * D * D,
            bytes_accessed=5_000_000,
            transcendentals=18 * 64 * 64,
        ),
    )(
        tokens,
        norm_gain,
        norm_shift,
        jnp.transpose(w_qkv, (1, 2, 0)).reshape(3 * HD, D),
        output_weight,
    )
    core = lax.axis_index("head") % 2
    return lax.dynamic_slice_in_dim(rows, 2 * core, 18, axis=1).astype(BF16)


def solution(mesh):
    return jax.shard_map(
        on_device,
        mesh=mesh,
        in_specs=(P("tm", None, None), P(), P(), P(None, "head", None), P("head", None)),
        out_specs=P("tm", "head", None),
        check_vma=False,
    )
```

```python
import math

import jax
import jax.numpy as jnp
from jax import lax
from jax.experimental import pallas as pl
from jax.experimental.pallas import tpu as pltpu
from jax.sharding import PartitionSpec as P

MESH = pl.DeviceIdType.MESH
D = 1408
HD = 88
FR = 4
PATCHES = 288
NT = 16
NH = 16
NZ = 8
HALF = PATCHES // 2
BLOCKS = 8
QA, QB = 5, 4
TA, TB = 2 * QA + 1, 2 * QB + 1
QFIRST = 3
TFIRST = 2 * QFIRST + 1
RT = 4
WROWS = 96
F32 = jnp.float32
BF16 = jnp.bfloat16


def kernel(
    tok_hbm, gain_row, shift_row, wq_hbm, wo_hbm, out,
    tok, wq, wo, wperm, packed, send, recv, ret_send, ret_recv, wbuf, rows_out,
    tok_sem, in_sem, p1_send, p1_recv, rt_send, rt_recv, w_send, w_recv,
):
    t = lax.axis_index("tm")
    h = lax.axis_index("head")
    xh, z = t // NZ, t % NZ
    chip, core = h // 2, h % 2
    y, xl = chip // 2, chip % 2
    is_a = xh == core

    halves = ((z + xl) % 2, (z + xl + 1) % 2)

    def z_of(block, y_, xl_):
        return ((block % 4 - y_ + 4) % 4) * 2 + (block // 4 + xl_) % 2

    def half_rows(n):
        return pl.ds(pl.multiple_of(halves[n] * HALF, 16), HALF)

    tok_copies = [
        pltpu.make_async_copy(
            tok_hbm.at[:, half_rows(n), :], tok.at[:, half_rows(n), :], tok_sem.at[n]
        )
        for n in range(2)
    ]
    wq_copy = pltpu.make_async_copy(wq_hbm, wq, in_sem.at[0])
    wo_copy = pltpu.make_async_copy(wo_hbm, wo, in_sem.at[1])
    tok_copies[0].start()
    wq_copy.start()
    tok_copies[1].start()
    wo_copy.start()

    def head_of(y_, xl_, core_):
        return ((y_ + 4) % 4) * 4 + xl_ * 2 + core_

    x_cross = ((1 - xh) * NZ + z, head_of(y, 1 - xl, core))
    barrier = pltpu.get_barrier_semaphore()

    @pl.loop(1, NT)
    def _(k):
        pl.semaphore_signal(barrier, inc=1, device_id=((t + k) % NT, h), device_id_type=MESH)
        pl.semaphore_signal(barrier, inc=1, device_id=(t, (h + k) % NH), device_id_type=MESH)

    pl.semaphore_signal(barrier, inc=1, device_id=x_cross, device_id_type=MESH)

    wq_copy.wait()
    w = wq[...].astype(F32)
    wperm[...] = jnp.concatenate(
        [w[0:88], w[176:216], w[88:176], w[216:264], jnp.zeros((120, D), F32)], axis=0
    ).astype(BF16)
    gain = gain_row[...].reshape(1, D)
    shift = shift_row[...].reshape(1, D)

    def project(n):
        tok_copies[n].wait()

        @pl.loop(0, FR)
        def _(f):
            values = tok[f, half_rows(n), :].astype(F32)
            average = jnp.mean(values, axis=-1, keepdims=True)
            centred = values - average
            var = jnp.mean(centred * centred, axis=-1, keepdims=True)
            normed = centred * lax.rsqrt(var + 1e-06) * gain + shift
            tok[f, half_rows(n), :] = normed.astype(BF16)

        packed[...] = lax.dot_general(
            tok[:, half_rows(n), :].reshape(FR * HALF, D), wperm[...],
            (((1,), (1,)), ((), ())), preferred_element_type=F32,
        ).reshape(FR, HALF, 384)

        parts = [packed[f].reshape(HALF // 8, 8, 384) for f in range(FR)]
        low = lax.broadcasted_iota(jnp.int32, parts[0].shape, 1) < 4
        turned = [pltpu.roll(part, 4, 1) for part in parts]
        even = jnp.concatenate(
            [jnp.where(low, parts[0], turned[1]), jnp.where(low, parts[2], turned[3])], axis=1
        )
        odd = jnp.concatenate(
            [jnp.where(low, turned[0], parts[1]), jnp.where(low, turned[2], parts[3])], axis=1
        )
        for b in range(BLOCKS // 2):
            for kind, first, count in ((0, 0, QA), (1, QA, QB)):
                rest = None
                for j in range(count):
                    q = 9 * b + first + j
                    tile = (odd if q % 2 else even)[q // 2]
                    at = halves[n] * (BLOCKS // 2) + b
                    send[at, kind, 1 + 2 * j] = tile[:, 0:128].astype(BF16)
                    send[at, kind, 2 + 2 * j] = tile[:, 128:256].astype(BF16)
                    left = tile[:, 256:384]
                    if j:
                        left = pltpu.roll(left, 8 * j, 1)
                    rest = left if rest is None else rest + left
                send[at, kind, 0] = rest.astype(BF16)

    def p1_to(b, kind):
        return jnp.where(kind == 0, core, 1 - core) * NZ + z_of(b, y, xl)

    def p1_copy(b, kind, group, tiles):
        src, dst = send.at[b, kind, tiles], recv.at[t, tiles]
        to_t = p1_to(b, kind)
        remote = pltpu.make_async_remote_copy(
            src_ref=src, dst_ref=dst, send_sem=p1_send.at[group, 2 * b + kind],
            recv_sem=p1_recv.at[group], device_id=(to_t, h), device_id_type=MESH,
        )
        return to_t == t, remote, lambda: pltpu.make_async_copy(src, dst, p1_recv.at[group])

    def start(triple):
        own, remote, local = triple

        @pl.when(own)
        def _():
            local().start()

        @pl.when(jnp.logical_not(own))
        def _():
            remote.start()

    def finish(triple):
        own, remote, _ = triple

        @pl.when(jnp.logical_not(own))
        def _():
            remote.wait_send()

    def p1_first(b, kind):
        return p1_copy(b, kind, 0, FIRST)

    def p1_second(b, kind):
        return p1_copy(b, kind, 1, SECOND[kind])

    FIRST = pl.ds(0, TFIRST)
    SECOND = (pl.ds(TFIRST, TA - TFIRST), pl.ds(TFIRST, TB - TFIRST))

    def block_at(n, step):
        off = step + 2 if n == 0 else step + 1 + z % 2
        return halves[n] * (BLOCKS // 2) + (z // 2 + off + y) % (BLOCKS // 2)

    def start_first(n):
        @pl.loop(0, BLOCKS // 2)
        def _(step):
            b = block_at(n, step)
            start(p1_first(b, jnp.where(is_a, 1, 0)))
            start(p1_first(b, jnp.where(is_a, 0, 1)))

    def start_second(n):
        @pl.loop(0, BLOCKS // 2)
        def _(step):
            b = block_at(n, step)
            start(p1_second(b, 0))
            start(p1_second(b, 1))

    sib = (t, chip * 2 + 1 - core)
    x_near = (t, head_of(y, 1 - xl, core))
    y_up, y_down = (t, head_of(y + 1, xl, core)), (t, head_of(y - 1, xl, core))
    slot_x = head_of(y, 1 - xl, core)
    FULL, LOW, HIGH = (0, WROWS), (0, WROWS // 2), (WROWS // 2, WROWS // 2)

    def w_copy(slot, rows, to, n_send, n_recv):
        ref = wbuf.at[slot, pl.ds(rows[0], rows[1]), :]
        return pltpu.make_async_remote_copy(
            src_ref=ref, dst_ref=ref, send_sem=w_send.at[n_send], recv_sem=w_recv.at[n_recv],
            device_id=to, device_id_type=MESH,
        )

    def slot(dy, other_x, other_core):
        return head_of(y + dy, (1 - xl) if other_x else xl, (1 - core) if other_core else core)

    w_sends = []

    def w_start(copy):
        copy.start()
        w_sends.append(copy)

    def w_wait(slot_, rows, n_recv):
        w_copy(slot_, rows, sib, 0, n_recv).wait_recv()

    def w_first():
        w_start(w_copy(h, LOW, x_near, 0, 8))
        w_start(w_copy(h, HIGH, x_cross, 1, 9))
        w_start(w_copy(h, FULL, y_up, 2, 10))
        w_start(w_copy(h, FULL, y_down, 3, 11))
        w_start(w_copy(h, FULL, sib, 4, 0))

    def w_second():
        w_wait(slot_x, LOW, 8)
        w_wait(slot_x, HIGH, 9)
        w_start(w_copy(slot_x, FULL, y_up, 5, 12))
        w_start(w_copy(slot_x, FULL, y_down, 6, 13))
        w_start(w_copy(slot_x, FULL, sib, 7, 1))

    def w_relay(other_x):
        for n, (dy, rows, to) in enumerate(((-1, LOW, y_up), (1, HIGH, y_down))):
            n += 2 * other_x
            at = slot(dy, other_x, 0)
            w_wait(at, FULL, 10 + n)
            w_start(w_copy(at, rows, to, 8 + n, 14 + n))
            w_start(w_copy(at, FULL, sib, 12 + n, 2 + n))

    def w_fourth():
        for other_x in (0, 1):
            at = slot(2, other_x, 0)
            w_wait(at, LOW, 14 + 2 * other_x)
            w_wait(at, HIGH, 15 + 2 * other_x)
            w_start(w_copy(at, FULL, sib, 16 + other_x, 6 + other_x))

    def w_last():
        for n, (dy, other_x) in enumerate(
            ((0, 0), (0, 1), (-1, 0), (1, 0), (-1, 1), (1, 1), (2, 0), (2, 1))
        ):
            w_wait(slot(dy, other_x, 1), FULL, n)

    project(0)
    pl.semaphore_wait(barrier, 2 * (NT - 1) + 1)
    start_first(0)
    wo_copy.wait()
    wbuf[h, pl.ds(0, WROWS), :] = jnp.concatenate(
        [wo[...].astype(F32), jnp.zeros((WROWS - HD, D), F32)], axis=0
    ).astype(BF16)

    @pl.loop(0, NH)
    def _(k):
        wbuf[k, pl.ds(WROWS, 128 - WROWS), :] = jnp.zeros((128 - WROWS, D), BF16)

    w_first()
    project(1)
    start_first(1)
    start_second(0)
    start_second(1)
    w_second()
    w_relay(0)

    def p1_wait(group, tiles):
        ref = recv.at[:, tiles]
        pltpu.make_async_copy(ref, ref, p1_recv.at[group]).wait()

    rows = 16 * NT
    lane = lax.broadcasted_iota(jnp.int32, (rows, 128), 1)
    same = (
        lax.broadcasted_iota(jnp.int32, (rows, rows), 0) % 4
        == lax.broadcasted_iota(jnp.int32, (rows, rows), 1) % 4
    )

    def attend(j):
        first = recv[:, 1 + 2 * j].reshape(rows, 128)
        second = recv[:, 2 + 2 * j].reshape(rows, 128)
        rest = recv[:, 0].reshape(rows, 128)
        scores = lax.dot_general(
            first[:, :HD], second[:, :HD], (((1,), (1,)), ((), ())), preferred_element_type=F32
        ) * (1.0 / math.sqrt(HD))
        scores = jnp.where(same, scores, -jnp.inf)
        exponent = jnp.exp(scores - jnp.max(scores, axis=-1, keepdims=True))
        probs = (exponent / jnp.sum(exponent, axis=-1, keepdims=True)).astype(BF16)
        values = jnp.concatenate([first, second, rest], axis=1)
        mixed = jnp.dot(probs, values, preferred_element_type=F32)
        return mixed

    def in_order(first, second, rest, turn):
        return jnp.where(
            lane < 40,
            pltpu.roll(first, 40, 1),
            jnp.where(lane < 80, pltpu.roll(second, 80, 1), pltpu.roll(rest, turn, 1)),
        )

    def straight(mixed, j):
        return in_order(
            mixed[:, 0:128], mixed[:, 128:256], mixed[:, 256:384], (80 - 8 * j) % 128
        )

    def put(n, tile):
        ret_send[:, n] = tile.astype(BF16).reshape(NT, 16, 128)

    to_chip = ((z + xl) % 2) * 4 + (z // 2 + y) % 4

    def ret_copy(to_t, to_core, first, count, sem):
        tiles = pl.ds(first, count)
        to_h = to_chip * 2 + to_core
        own = jnp.logical_and(to_t == t, to_h == h)
        src, dst = ret_send.at[to_t, tiles], ret_recv.at[h, tiles]
        remote = pltpu.make_async_remote_copy(
            src_ref=src, dst_ref=dst, send_sem=rt_send.at[sem, to_t], recv_sem=rt_recv.at[0],
            device_id=(to_t, to_h), device_id_type=MESH,
        )
        return own, remote, lambda: pltpu.make_async_copy(src, dst, rt_recv.at[0])

    def far_first(k):
        n, away = k // 2, (k // 2 + 1) // 2
        off = jnp.where(n % 2 == 0, NZ // 2 - away, NZ // 2 + away)
        return ((xh + 1 - k % 2) % 2) * NZ + (z + off) % NZ

    def ret_first(to_t):
        return ret_copy(to_t, jnp.where(is_a, 0, 1), 0, 2, 0)

    def ret_second_a(to_t):
        return ret_copy(to_t, 0, 2, 2, 1)

    def ret_second_b(to_t):
        return ret_copy(to_t, 1, 2, 1, 1)

    def ret_shared(to_t):
        return ret_copy(to_t, 1, 3, 1, 2)

    p1_wait(0, FIRST)

    mixed2 = attend(2)
    put(0, jnp.where(lane < HD, straight(attend(0), 0), mixed2[:, 0:128]))
    put(1, jnp.where(lane < HD, straight(attend(1), 1), mixed2[:, 128:256]))
    rest2 = pltpu.roll(mixed2[:, 256:384], 72, 1)

    @pl.loop(0, NT)
    def _(k):
        start(ret_first(far_first(k)))

    w_relay(1)

    @pl.when(is_a)
    def _():
        p1_wait(1, SECOND[0])
        put(3, straight(attend(4), 4))

    @pl.when(jnp.logical_not(is_a))
    def _():
        p1_wait(1, SECOND[1])

    put(2, jnp.where(lane < HD, straight(attend(3), 3), rest2))

    @pl.when(is_a)
    def _():
        @pl.loop(0, NT)
        def _(k):
            to_t = far_first(k)
            start(ret_second_a(to_t))
            start(ret_shared(to_t))

    @pl.when(jnp.logical_not(is_a))
    def _():
        @pl.loop(0, NT)
        def _(k):
            start(ret_second_b(far_first(k)))

    w_fourth()
    w_last()

    @pl.loop(0, BLOCKS)
    def _(b):
        for kind in range(2):
            finish(p1_first(b, kind))
            finish(p1_second(b, kind))

    @pl.loop(0, NT)
    def _(to_t):
        finish(ret_first(to_t))

    @pl.when(is_a)
    def _():
        @pl.loop(0, NT)
        def _(to_t):
            finish(ret_second_a(to_t))
            finish(ret_shared(to_t))

    @pl.when(jnp.logical_not(is_a))
    def _():
        @pl.loop(0, NT)
        def _(to_t):
            finish(ret_second_b(to_t))

    for copy in w_sends:
        copy.wait_send()

    pltpu.make_async_copy(ret_recv, ret_recv, rt_recv.at[0]).wait()

    tiles = [ret_recv[:, n] for n in range(RT)]
    parts = [tile.reshape(rows, 128).astype(F32) for tile in tiles[:3]]
    third = in_order(parts[0], parts[1], parts[2], 120).astype(BF16).reshape(NH, 16, 128)
    left = jnp.concatenate(
        [
            jnp.concatenate([quad[g] for g in range(NH)], axis=1)
            for quad in (tiles[0], tiles[1], third, tiles[2], tiles[3])
        ],
        axis=0,
    )
    total = jnp.dot(left, wbuf[...].reshape(NH * 128, D), preferred_element_type=F32)

    rows_out[...] = total.reshape(QA, 2, 8, D)
    low = lax.broadcasted_iota(jnp.int32, (8, D), 0) < 4
    for f in range(FR):
        for pair in range(3):
            lo = rows_out[(2 * pair + QA - core) % QA, f // 2]
            hi = rows_out[(2 * pair + 1 + QA - core) % QA, f // 2] if pair < 2 else lo
            if f % 2 == 0:
                rows_ = jnp.where(low, lo, pltpu.roll(hi, 4, 0))
            else:
                rows_ = jnp.where(low, pltpu.roll(lo, 4, 0), hi)
            out[f, pl.ds(8 * pair, 8), :] = rows_


def on_device(tokens, norm_gain, norm_shift, w_qkv, output_weight):
    vmem = pl.BlockSpec(memory_space=pltpu.VMEM)
    hbm = pl.BlockSpec(memory_space=pl.ANY)
    dma = pltpu.SemaphoreType.DMA
    rows = pl.pallas_call(
        kernel,
        out_shape=jax.ShapeDtypeStruct((FR, 24, D), F32),
        in_specs=[hbm, vmem, vmem, hbm, hbm],
        out_specs=vmem,
        scratch_shapes=[
            pltpu.VMEM((FR, PATCHES, D), BF16),
            pltpu.VMEM((3 * HD, D), BF16),
            pltpu.VMEM((HD, D), BF16),
            pltpu.VMEM((384, D), BF16),
            pltpu.VMEM((FR, HALF, 384), F32),
            pltpu.VMEM((BLOCKS, 2, TA, 16, 128), BF16),
            pltpu.VMEM((NT, TA, 16, 128), BF16),
            pltpu.VMEM((NT, RT, 16, 128), BF16),
            pltpu.VMEM((NH, RT, 16, 128), BF16),
            pltpu.VMEM((NH, 128, D), BF16),
            pltpu.VMEM((QA, 2, 8, D), F32),
            dma((2,)),
            dma((2,)),
            dma((2, 2 * BLOCKS)),
            dma((2,)),
            dma((3, NT)),
            dma((1,)),
            dma((18,)),
            dma((18,)),
        ],
        compiler_params=pltpu.CompilerParams(
            collective_id=0, has_side_effects=True, vmem_limit_bytes=60 * 1024 * 1024
        ),
        cost_estimate=pl.CostEstimate(
            flops=2 * FR * PATCHES * D * 264 + 2 * 72 * D * D,
            bytes_accessed=5_000_000,
            transcendentals=18 * 64 * 64,
        ),
    )(
        tokens,
        norm_gain,
        norm_shift,
        jnp.transpose(w_qkv, (1, 2, 0)).reshape(3 * HD, D),
        output_weight,
    )
    core = lax.axis_index("head") % 2
    return lax.dynamic_slice_in_dim(rows, 2 * core, 18, axis=1).astype(BF16)


def solution(mesh):
    return jax.shard_map(
        on_device,
        mesh=mesh,
        in_specs=(P("tm", None, None), P(), P(), P(None, "head", None), P("head", None)),
        out_specs=P("tm", "head", None),
        check_vma=False,
    )
```

```python
import math

import jax
import jax.numpy as jnp
from jax import lax
from jax.experimental import pallas as pl
from jax.experimental.pallas import tpu as pltpu
from jax.sharding import PartitionSpec as P

MESH = pl.DeviceIdType.MESH
D = 1408
HD = 88
FR = 4
PATCHES = 288
NT = 16
NH = 16
NZ = 8
HALF = PATCHES // 2
BLOCKS = 8
QA, QB = 5, 4
TA, TB = 2 * QA + 1, 2 * QB + 1
QFIRST = 3
TFIRST = 2 * QFIRST + 1
RT = 4
WROWS = 96
F32 = jnp.float32
BF16 = jnp.bfloat16


def kernel(
    tok_hbm, gain_hbm, shift_hbm, wq_hbm, wo_hbm, out,
    tok, gain_row, shift_row, wq, wo, wperm, packed, send, recv, ret_send, ret_recv, wbuf, rows_out,
    tok_sem, in_sem, p1_send, p1_recv, rt_send, rt_recv, w_send, w_recv,
):
    t = lax.axis_index("tm")
    h = lax.axis_index("head")
    xh, z = t // NZ, t % NZ
    chip, core = h // 2, h % 2
    y, xl = chip // 2, chip % 2
    is_a = xh == core

    halves = ((z + xl) % 2, (z + xl + 1) % 2)

    def z_of(block, y_, xl_):
        return ((block % 4 - y_ + 4) % 4) * 2 + (block // 4 + xl_) % 2

    def half_rows(n):
        return pl.ds(pl.multiple_of(halves[n] * HALF, 16), HALF)

    tok_copies = [
        pltpu.make_async_copy(
            tok_hbm.at[:, half_rows(n), :], tok.at[:, half_rows(n), :], tok_sem.at[n]
        )
        for n in range(2)
    ]
    wq_copy = pltpu.make_async_copy(wq_hbm, wq, in_sem.at[0])
    wo_copy = pltpu.make_async_copy(wo_hbm, wo, in_sem.at[1])
    gain_copy = pltpu.make_async_copy(gain_hbm, gain_row, in_sem.at[2])
    shift_copy = pltpu.make_async_copy(shift_hbm, shift_row, in_sem.at[3])
    tok_copies[0].start()
    wq_copy.start()
    gain_copy.start()
    shift_copy.start()
    tok_copies[1].start()
    wo_copy.start()

    def head_of(y_, xl_, core_):
        return ((y_ + 4) % 4) * 4 + xl_ * 2 + core_

    x_cross = ((1 - xh) * NZ + z, head_of(y, 1 - xl, core))
    barrier = pltpu.get_barrier_semaphore()

    @pl.loop(1, NT)
    def _(k):
        pl.semaphore_signal(barrier, inc=1, device_id=((t + k) % NT, h), device_id_type=MESH)
        pl.semaphore_signal(barrier, inc=1, device_id=(t, (h + k) % NH), device_id_type=MESH)

    pl.semaphore_signal(barrier, inc=1, device_id=x_cross, device_id_type=MESH)

    wq_copy.wait()
    w = wq[...].astype(F32)
    wperm[...] = jnp.concatenate(
        [w[0:88], w[176:216], w[88:176], w[216:264], jnp.zeros((120, D), F32)], axis=0
    ).astype(BF16)
    gain_copy.wait()
    shift_copy.wait()
    gain = gain_row[...].reshape(1, D)
    shift = shift_row[...].reshape(1, D)

    def project(n):
        tok_copies[n].wait()

        @pl.loop(0, FR)
        def _(f):
            values = tok[f, half_rows(n), :].astype(F32)
            average = jnp.mean(values, axis=-1, keepdims=True)
            centred = values - average
            var = jnp.mean(centred * centred, axis=-1, keepdims=True)
            normed = centred * lax.rsqrt(var + 1e-06) * gain + shift
            tok[f, half_rows(n), :] = normed.astype(BF16)

        packed[...] = lax.dot_general(
            tok[:, half_rows(n), :].reshape(FR * HALF, D), wperm[...],
            (((1,), (1,)), ((), ())), preferred_element_type=F32,
        ).reshape(FR, HALF, 384)

        parts = [packed[f].reshape(HALF // 8, 8, 384) for f in range(FR)]
        low = lax.broadcasted_iota(jnp.int32, parts[0].shape, 1) < 4
        turned = [pltpu.roll(part, 4, 1) for part in parts]
        even = jnp.concatenate(
            [jnp.where(low, parts[0], turned[1]), jnp.where(low, parts[2], turned[3])], axis=1
        )
        odd = jnp.concatenate(
            [jnp.where(low, turned[0], parts[1]), jnp.where(low, turned[2], parts[3])], axis=1
        )
        for b in range(BLOCKS // 2):
            for kind, first, count in ((0, 0, QA), (1, QA, QB)):
                rest = None
                for j in range(count):
                    q = 9 * b + first + j
                    tile = (odd if q % 2 else even)[q // 2]
                    at = halves[n] * (BLOCKS // 2) + b
                    send[at, kind, 1 + 2 * j] = tile[:, 0:128].astype(BF16)
                    send[at, kind, 2 + 2 * j] = tile[:, 128:256].astype(BF16)
                    left = tile[:, 256:384]
                    if j:
                        left = pltpu.roll(left, 8 * j, 1)
                    rest = left if rest is None else rest + left
                send[at, kind, 0] = rest.astype(BF16)

    def p1_to(b, kind):
        return jnp.where(kind == 0, core, 1 - core) * NZ + z_of(b, y, xl)

    def p1_copy(b, kind, group, tiles):
        src, dst = send.at[b, kind, tiles], recv.at[t, tiles]
        to_t = p1_to(b, kind)
        remote = pltpu.make_async_remote_copy(
            src_ref=src, dst_ref=dst, send_sem=p1_send.at[group, 2 * b + kind],
            recv_sem=p1_recv.at[group], device_id=(to_t, h), device_id_type=MESH,
        )
        return to_t == t, remote, lambda: pltpu.make_async_copy(src, dst, p1_recv.at[group])

    def start(triple):
        own, remote, local = triple

        @pl.when(own)
        def _():
            local().start()

        @pl.when(jnp.logical_not(own))
        def _():
            remote.start()

    def finish(triple):
        own, remote, _ = triple

        @pl.when(jnp.logical_not(own))
        def _():
            remote.wait_send()

    def p1_first(b, kind):
        return p1_copy(b, kind, 0, FIRST)

    def p1_second(b, kind):
        return p1_copy(b, kind, 1, SECOND[kind])

    FIRST = pl.ds(0, TFIRST)
    SECOND = (pl.ds(TFIRST, TA - TFIRST), pl.ds(TFIRST, TB - TFIRST))

    def block_at(n, step):
        off = step + 2 if n == 0 else step + 1 + z % 2
        return halves[n] * (BLOCKS // 2) + (z // 2 + off + y) % (BLOCKS // 2)

    def start_first(n):
        @pl.loop(0, BLOCKS // 2)
        def _(step):
            b = block_at(n, step)
            start(p1_first(b, jnp.where(is_a, 1, 0)))
            start(p1_first(b, jnp.where(is_a, 0, 1)))

    def start_second(n):
        @pl.loop(0, BLOCKS // 2)
        def _(step):
            b = block_at(n, step)
            start(p1_second(b, 0))
            start(p1_second(b, 1))

    sib = (t, chip * 2 + 1 - core)
    x_near = (t, head_of(y, 1 - xl, core))
    y_up, y_down = (t, head_of(y + 1, xl, core)), (t, head_of(y - 1, xl, core))
    slot_x = head_of(y, 1 - xl, core)
    FULL, LOW, HIGH = (0, WROWS), (0, WROWS // 2), (WROWS // 2, WROWS // 2)

    def w_copy(slot, rows, to, n_send, n_recv):
        ref = wbuf.at[slot, pl.ds(rows[0], rows[1]), :]
        return pltpu.make_async_remote_copy(
            src_ref=ref, dst_ref=ref, send_sem=w_send.at[n_send], recv_sem=w_recv.at[n_recv],
            device_id=to, device_id_type=MESH,
        )

    def slot(dy, other_x, other_core):
        return head_of(y + dy, (1 - xl) if other_x else xl, (1 - core) if other_core else core)

    w_sends = []

    def w_start(copy):
        copy.start()
        w_sends.append(copy)

    def w_wait(slot_, rows, n_recv):
        w_copy(slot_, rows, sib, 0, n_recv).wait_recv()

    def w_first():
        w_start(w_copy(h, LOW, x_near, 0, 8))
        w_start(w_copy(h, HIGH, x_cross, 1, 9))
        w_start(w_copy(h, FULL, y_up, 2, 10))
        w_start(w_copy(h, FULL, y_down, 3, 11))
        w_start(w_copy(h, FULL, sib, 4, 0))

    def w_second():
        w_wait(slot_x, LOW, 8)
        w_wait(slot_x, HIGH, 9)
        w_start(w_copy(slot_x, FULL, y_up, 5, 12))
        w_start(w_copy(slot_x, FULL, y_down, 6, 13))
        w_start(w_copy(slot_x, FULL, sib, 7, 1))

    def w_relay(other_x):
        for n, (dy, rows, to) in enumerate(((-1, LOW, y_up), (1, HIGH, y_down))):
            n += 2 * other_x
            at = slot(dy, other_x, 0)
            w_wait(at, FULL, 10 + n)
            w_start(w_copy(at, rows, to, 8 + n, 14 + n))
            w_start(w_copy(at, FULL, sib, 12 + n, 2 + n))

    def w_fourth():
        for other_x in (0, 1):
            at = slot(2, other_x, 0)
            w_wait(at, LOW, 14 + 2 * other_x)
            w_wait(at, HIGH, 15 + 2 * other_x)
            w_start(w_copy(at, FULL, sib, 16 + other_x, 6 + other_x))

    def w_last():
        for n, (dy, other_x) in enumerate(
            ((0, 0), (0, 1), (-1, 0), (1, 0), (-1, 1), (1, 1), (2, 0), (2, 1))
        ):
            w_wait(slot(dy, other_x, 1), FULL, n)

    project(0)
    pl.semaphore_wait(barrier, 2 * (NT - 1) + 1)
    start_first(0)
    wo_copy.wait()
    wbuf[h, pl.ds(0, WROWS), :] = jnp.concatenate(
        [wo[...].astype(F32), jnp.zeros((WROWS - HD, D), F32)], axis=0
    ).astype(BF16)

    @pl.loop(0, NH)
    def _(k):
        wbuf[k, pl.ds(WROWS, 128 - WROWS), :] = jnp.zeros((128 - WROWS, D), BF16)

    w_first()
    project(1)
    start_first(1)
    start_second(0)
    start_second(1)
    w_second()
    w_relay(0)

    def p1_wait(group, tiles):
        ref = recv.at[:, tiles]
        pltpu.make_async_copy(ref, ref, p1_recv.at[group]).wait()

    rows = 16 * NT
    lane = lax.broadcasted_iota(jnp.int32, (rows, 128), 1)
    same = (
        lax.broadcasted_iota(jnp.int32, (rows, rows), 0) % 4
        == lax.broadcasted_iota(jnp.int32, (rows, rows), 1) % 4
    )

    def attend(j):
        first = recv[:, 1 + 2 * j].reshape(rows, 128)
        second = recv[:, 2 + 2 * j].reshape(rows, 128)
        rest = recv[:, 0].reshape(rows, 128)
        scores = lax.dot_general(
            first[:, :HD], second[:, :HD], (((1,), (1,)), ((), ())), preferred_element_type=F32
        ) * (1.0 / math.sqrt(HD))
        scores = jnp.where(same, scores, -jnp.inf)
        exponent = jnp.exp(scores - jnp.max(scores, axis=-1, keepdims=True))
        probs = (exponent / jnp.sum(exponent, axis=-1, keepdims=True)).astype(BF16)
        values = jnp.concatenate([first, second, rest], axis=1)
        mixed = jnp.dot(probs, values, preferred_element_type=F32)
        return mixed

    def in_order(first, second, rest, turn):
        return jnp.where(
            lane < 40,
            pltpu.roll(first, 40, 1),
            jnp.where(lane < 80, pltpu.roll(second, 80, 1), pltpu.roll(rest, turn, 1)),
        )

    def straight(mixed, j):
        return in_order(
            mixed[:, 0:128], mixed[:, 128:256], mixed[:, 256:384], (80 - 8 * j) % 128
        )

    def put(n, tile):
        ret_send[:, n] = tile.astype(BF16).reshape(NT, 16, 128)

    to_chip = ((z + xl) % 2) * 4 + (z // 2 + y) % 4

    def ret_copy(to_t, to_core, first, count, sem):
        tiles = pl.ds(first, count)
        to_h = to_chip * 2 + to_core
        own = jnp.logical_and(to_t == t, to_h == h)
        src, dst = ret_send.at[to_t, tiles], ret_recv.at[h, tiles]
        remote = pltpu.make_async_remote_copy(
            src_ref=src, dst_ref=dst, send_sem=rt_send.at[sem, to_t], recv_sem=rt_recv.at[0],
            device_id=(to_t, to_h), device_id_type=MESH,
        )
        return own, remote, lambda: pltpu.make_async_copy(src, dst, rt_recv.at[0])

    def far_first(k):
        n, away = k // 2, (k // 2 + 1) // 2
        off = jnp.where(n % 2 == 0, NZ // 2 - away, NZ // 2 + away)
        return ((xh + 1 - k % 2) % 2) * NZ + (z + off) % NZ

    def ret_first(to_t):
        return ret_copy(to_t, jnp.where(is_a, 0, 1), 0, 2, 0)

    def ret_second_a(to_t):
        return ret_copy(to_t, 0, 2, 2, 1)

    def ret_second_b(to_t):
        return ret_copy(to_t, 1, 2, 1, 1)

    def ret_shared(to_t):
        return ret_copy(to_t, 1, 3, 1, 2)

    p1_wait(0, FIRST)

    mixed2 = attend(2)
    put(0, jnp.where(lane < HD, straight(attend(0), 0), mixed2[:, 0:128]))
    put(1, jnp.where(lane < HD, straight(attend(1), 1), mixed2[:, 128:256]))
    rest2 = pltpu.roll(mixed2[:, 256:384], 72, 1)

    @pl.loop(0, NT)
    def _(k):
        start(ret_first(far_first(k)))

    w_relay(1)

    @pl.when(is_a)
    def _():
        p1_wait(1, SECOND[0])
        put(3, straight(attend(4), 4))

    @pl.when(jnp.logical_not(is_a))
    def _():
        p1_wait(1, SECOND[1])

    put(2, jnp.where(lane < HD, straight(attend(3), 3), rest2))

    @pl.when(is_a)
    def _():
        @pl.loop(0, NT)
        def _(k):
            to_t = far_first(k)
            start(ret_second_a(to_t))
            start(ret_shared(to_t))

    @pl.when(jnp.logical_not(is_a))
    def _():
        @pl.loop(0, NT)
        def _(k):
            start(ret_second_b(far_first(k)))

    w_fourth()
    w_last()

    @pl.loop(0, BLOCKS)
    def _(b):
        for kind in range(2):
            finish(p1_first(b, kind))
            finish(p1_second(b, kind))

    @pl.loop(0, NT)
    def _(to_t):
        finish(ret_first(to_t))

    @pl.when(is_a)
    def _():
        @pl.loop(0, NT)
        def _(to_t):
            finish(ret_second_a(to_t))
            finish(ret_shared(to_t))

    @pl.when(jnp.logical_not(is_a))
    def _():
        @pl.loop(0, NT)
        def _(to_t):
            finish(ret_second_b(to_t))

    for copy in w_sends:
        copy.wait_send()

    pltpu.make_async_copy(ret_recv, ret_recv, rt_recv.at[0]).wait()

    tiles = [ret_recv[:, n] for n in range(RT)]
    parts = [tile.reshape(rows, 128).astype(F32) for tile in tiles[:3]]
    third = in_order(parts[0], parts[1], parts[2], 120).astype(BF16).reshape(NH, 16, 128)
    left = jnp.concatenate(
        [
            jnp.concatenate([quad[g] for g in range(NH)], axis=1)
            for quad in (tiles[0], tiles[1], third, tiles[2], tiles[3])
        ],
        axis=0,
    )
    total = jnp.dot(left, wbuf[...].reshape(NH * 128, D), preferred_element_type=F32)

    for c in range(D // 128):
        rows_out[c] = total[:, 128 * c : 128 * c + 128]
    for o in range(18):
        at = o + 2 * core
        quad = (at // 4 + QA - core) % QA
        for c in range(D // 128):
            out[o, :, pl.ds(128 * c, 128)] = rows_out[
                c, pl.ds(16 * quad + at % 4, FR, stride=4), :
            ].astype(BF16)


def on_device(tokens, norm_gain, norm_shift, w_qkv, output_weight):
    vmem = pl.BlockSpec(memory_space=pltpu.VMEM)
    hbm = pl.BlockSpec(memory_space=pl.ANY)
    dma = pltpu.SemaphoreType.DMA
    rows = pl.pallas_call(
        kernel,
        out_shape=jax.ShapeDtypeStruct((18, FR, D), BF16),
        in_specs=[hbm] * 5,
        out_specs=vmem,
        scratch_shapes=[
            pltpu.VMEM((FR, PATCHES, D), BF16),
            pltpu.VMEM((D,), F32),
            pltpu.VMEM((D,), F32),
            pltpu.VMEM((3 * HD, D), BF16),
            pltpu.VMEM((HD, D), BF16),
            pltpu.VMEM((384, D), BF16),
            pltpu.VMEM((FR, HALF, 384), F32),
            pltpu.VMEM((BLOCKS, 2, TA, 16, 128), BF16),
            pltpu.VMEM((NT, TA, 16, 128), BF16),
            pltpu.VMEM((NT, RT, 16, 128), BF16),
            pltpu.VMEM((NH, RT, 16, 128), BF16),
            pltpu.VMEM((NH, 128, D), BF16),
            pltpu.VMEM((D // 128, 16 * QA, 128), F32),
            dma((2,)),
            dma((4,)),
            dma((2, 2 * BLOCKS)),
            dma((2,)),
            dma((3, NT)),
            dma((1,)),
            dma((18,)),
            dma((18,)),
        ],
        compiler_params=pltpu.CompilerParams(
            collective_id=0, has_side_effects=True, vmem_limit_bytes=55000 * 1024
        ),
        cost_estimate=pl.CostEstimate(
            flops=2 * FR * PATCHES * D * 264 + 2 * 72 * D * D,
            bytes_accessed=5_000_000,
            transcendentals=18 * 64 * 64,
        ),
    )(
        tokens,
        norm_gain,
        norm_shift,
        jnp.transpose(w_qkv, (1, 2, 0)).reshape(3 * HD, D),
        output_weight,
    )
    return jnp.transpose(rows, (1, 0, 2))


def solution(mesh):
    return jax.shard_map(
        on_device,
        mesh=mesh,
        in_specs=(P("tm", None, None), P(), P(), P(None, "head", None), P("head", None)),
        out_specs=P("tm", "head", None),
        check_vma=False,
    )
```

```python
import math

import jax
import jax.numpy as jnp
from jax import lax
from jax.experimental import pallas as pl
from jax.experimental.pallas import tpu as pltpu
from jax.sharding import PartitionSpec as P

MESH = pl.DeviceIdType.MESH
D = 1408
HD = 88
FR = 4
PATCHES = 288
NT = 16
NH = 16
NZ = 8
HALF = PATCHES // 2
BLOCKS = 8
QA, QB = 5, 4
TA, TB = 2 * QA + 1, 2 * QB + 1
QFIRST = 3
TFIRST = 2 * QFIRST + 1
RT = 4
WROWS = 96
F32 = jnp.float32
BF16 = jnp.bfloat16


def kernel(
    tok_hbm, gain_hbm, shift_hbm, wq_hbm, wo_hbm, out,
    tok, gain_row, shift_row, wq, wo, wperm, packed, send, recv, ret_send, ret_recv, wbuf, rows_out,
    tok_sem, in_sem, p1_send, p1_recv, rt_send, rt_recv, w_send, w_recv,
):
    t = lax.axis_index("tm")
    h = lax.axis_index("head")
    xh, z = t // NZ, t % NZ
    chip, core = h // 2, h % 2
    y, xl = chip // 2, chip % 2
    is_a = xh == core

    halves = ((z + xl) % 2, (z + xl + 1) % 2)

    def z_of(block, y_, xl_):
        return ((block % 4 - y_ + 4) % 4) * 2 + (block // 4 + xl_) % 2

    def half_rows(n):
        return pl.ds(pl.multiple_of(halves[n] * HALF, 16), HALF)

    tok_copies = [
        pltpu.make_async_copy(
            tok_hbm.at[:, half_rows(n), :], tok.at[:, half_rows(n), :], tok_sem.at[n]
        )
        for n in range(2)
    ]
    wq_copy = pltpu.make_async_copy(wq_hbm, wq, in_sem.at[0])
    wo_copy = pltpu.make_async_copy(wo_hbm, wo, in_sem.at[1])
    gain_copy = pltpu.make_async_copy(gain_hbm, gain_row, in_sem.at[2])
    shift_copy = pltpu.make_async_copy(shift_hbm, shift_row, in_sem.at[3])
    tok_copies[0].start()
    wq_copy.start()
    gain_copy.start()
    shift_copy.start()
    tok_copies[1].start()
    wo_copy.start()

    def head_of(y_, xl_, core_):
        return ((y_ + 4) % 4) * 4 + xl_ * 2 + core_

    x_cross = ((1 - xh) * NZ + z, head_of(y, 1 - xl, core))
    barrier = pltpu.get_barrier_semaphore()

    @pl.loop(1, NT)
    def _(k):
        pl.semaphore_signal(barrier, inc=1, device_id=((t + k) % NT, h), device_id_type=MESH)
        pl.semaphore_signal(barrier, inc=1, device_id=(t, (h + k) % NH), device_id_type=MESH)

    pl.semaphore_signal(barrier, inc=1, device_id=x_cross, device_id_type=MESH)

    wq_copy.wait()
    w = wq[...].astype(F32)
    wperm[...] = jnp.concatenate(
        [w[0:88], w[176:216], w[88:176], w[216:264], jnp.zeros((120, D), F32)], axis=0
    ).astype(BF16)
    gain_copy.wait()
    shift_copy.wait()
    gain = gain_row[...].reshape(1, D)
    shift = shift_row[...].reshape(1, D)

    def project(n):
        tok_copies[n].wait()
        values = tok[:, half_rows(n), :].reshape(FR * HALF, D).astype(F32)
        average = jnp.mean(values, axis=-1, keepdims=True)
        centred = values - average
        var = jnp.mean(centred * centred, axis=-1, keepdims=True)
        normed = centred * lax.rsqrt(var + 1e-06) * gain + shift
        normed = normed.astype(BF16)

        packed[...] = lax.dot_general(
            normed, wperm[...],
            (((1,), (1,)), ((), ())), preferred_element_type=F32,
        ).reshape(FR, HALF, 384)

        parts = [packed[f].reshape(HALF // 8, 8, 384) for f in range(FR)]
        low = lax.broadcasted_iota(jnp.int32, parts[0].shape, 1) < 4
        turned = [pltpu.roll(part, 4, 1) for part in parts]
        even = jnp.concatenate(
            [jnp.where(low, parts[0], turned[1]), jnp.where(low, parts[2], turned[3])], axis=1
        )
        odd = jnp.concatenate(
            [jnp.where(low, turned[0], parts[1]), jnp.where(low, turned[2], parts[3])], axis=1
        )
        for b in range(BLOCKS // 2):
            for kind, first, count in ((0, 0, QA), (1, QA, QB)):
                rest = None
                for j in range(count):
                    q = 9 * b + first + j
                    tile = (odd if q % 2 else even)[q // 2]
                    at = halves[n] * (BLOCKS // 2) + b
                    send[at, kind, 1 + 2 * j] = tile[:, 0:128].astype(BF16)
                    send[at, kind, 2 + 2 * j] = tile[:, 128:256].astype(BF16)
                    left = tile[:, 256:384]
                    if j:
                        left = pltpu.roll(left, 8 * j, 1)
                    rest = left if rest is None else rest + left
                send[at, kind, 0] = rest.astype(BF16)

    def p1_to(b, kind):
        return jnp.where(kind == 0, core, 1 - core) * NZ + z_of(b, y, xl)

    def p1_copy(b, kind, group, tiles):
        src, dst = send.at[b, kind, tiles], recv.at[t, tiles]
        to_t = p1_to(b, kind)
        remote = pltpu.make_async_remote_copy(
            src_ref=src, dst_ref=dst, send_sem=p1_send.at[group, 2 * b + kind],
            recv_sem=p1_recv.at[group], device_id=(to_t, h), device_id_type=MESH,
        )
        return to_t == t, remote, lambda: pltpu.make_async_copy(src, dst, p1_recv.at[group])

    def start(triple):
        own, remote, local = triple

        @pl.when(own)
        def _():
            local().start()

        @pl.when(jnp.logical_not(own))
        def _():
            remote.start()

    def finish(triple):
        own, remote, _ = triple

        @pl.when(jnp.logical_not(own))
        def _():
            remote.wait_send()

    def p1_first(b, kind):
        return p1_copy(b, kind, 0, FIRST)

    def p1_second(b, kind):
        return p1_copy(b, kind, 1, SECOND[kind])

    FIRST = pl.ds(0, TFIRST)
    SECOND = (pl.ds(TFIRST, TA - TFIRST), pl.ds(TFIRST, TB - TFIRST))

    def block_at(n, step):
        off = step + 2 if n == 0 else step + 1 + z % 2
        return halves[n] * (BLOCKS // 2) + (z // 2 + off + y) % (BLOCKS // 2)

    def start_first(n):
        @pl.loop(0, BLOCKS // 2)
        def _(step):
            b = block_at(n, step)
            start(p1_first(b, jnp.where(is_a, 1, 0)))
            start(p1_first(b, jnp.where(is_a, 0, 1)))

    def start_second(n):
        @pl.loop(0, BLOCKS // 2)
        def _(step):
            b = block_at(n, step)
            start(p1_second(b, 0))
            start(p1_second(b, 1))

    sib = (t, chip * 2 + 1 - core)
    x_near = (t, head_of(y, 1 - xl, core))
    y_up, y_down = (t, head_of(y + 1, xl, core)), (t, head_of(y - 1, xl, core))
    slot_x = head_of(y, 1 - xl, core)
    FULL, LOW, HIGH = (0, WROWS), (0, WROWS // 2), (WROWS // 2, WROWS // 2)

    def w_copy(slot, rows, to, n_send, n_recv):
        ref = wbuf.at[slot, pl.ds(rows[0], rows[1]), :]
        return pltpu.make_async_remote_copy(
            src_ref=ref, dst_ref=ref, send_sem=w_send.at[n_send], recv_sem=w_recv.at[n_recv],
            device_id=to, device_id_type=MESH,
        )

    def slot(dy, other_x, other_core):
        return head_of(y + dy, (1 - xl) if other_x else xl, (1 - core) if other_core else core)

    w_sends = []

    def w_start(copy):
        copy.start()
        w_sends.append(copy)

    def w_wait(slot_, rows, n_recv):
        w_copy(slot_, rows, sib, 0, n_recv).wait_recv()

    def w_first():
        w_start(w_copy(h, LOW, x_near, 0, 8))
        w_start(w_copy(h, HIGH, x_cross, 1, 9))
        w_start(w_copy(h, FULL, y_up, 2, 10))
        w_start(w_copy(h, FULL, y_down, 3, 11))
        w_start(w_copy(h, FULL, sib, 4, 0))

    def w_second():
        w_wait(slot_x, LOW, 8)
        w_wait(slot_x, HIGH, 9)
        w_start(w_copy(slot_x, FULL, y_up, 5, 12))
        w_start(w_copy(slot_x, FULL, y_down, 6, 13))
        w_start(w_copy(slot_x, FULL, sib, 7, 1))

    def w_relay(other_x):
        for n, (dy, rows, to) in enumerate(((-1, LOW, y_up), (1, HIGH, y_down))):
            n += 2 * other_x
            at = slot(dy, other_x, 0)
            w_wait(at, FULL, 10 + n)
            w_start(w_copy(at, rows, to, 8 + n, 14 + n))
            w_start(w_copy(at, FULL, sib, 12 + n, 2 + n))

    def w_fourth():
        for other_x in (0, 1):
            at = slot(2, other_x, 0)
            w_wait(at, LOW, 14 + 2 * other_x)
            w_wait(at, HIGH, 15 + 2 * other_x)
            w_start(w_copy(at, FULL, sib, 16 + other_x, 6 + other_x))

    def w_last():
        for n, (dy, other_x) in enumerate(
            ((0, 0), (0, 1), (-1, 0), (1, 0), (-1, 1), (1, 1), (2, 0), (2, 1))
        ):
            w_wait(slot(dy, other_x, 1), FULL, n)

    project(0)
    pl.semaphore_wait(barrier, 2 * (NT - 1) + 1)
    start_first(0)
    wo_copy.wait()
    wbuf[h, pl.ds(0, WROWS), :] = jnp.concatenate(
        [wo[...].astype(F32), jnp.zeros((WROWS - HD, D), F32)], axis=0
    ).astype(BF16)

    @pl.loop(0, NH)
    def _(k):
        wbuf[k, pl.ds(WROWS, 128 - WROWS), :] = jnp.zeros((128 - WROWS, D), BF16)

    w_first()
    project(1)
    start_first(1)
    start_second(0)
    start_second(1)
    w_second()
    w_relay(0)

    def p1_wait(group, tiles):
        ref = recv.at[:, tiles]
        pltpu.make_async_copy(ref, ref, p1_recv.at[group]).wait()

    rows = 16 * NT
    lane = lax.broadcasted_iota(jnp.int32, (rows, 128), 1)
    same = (
        lax.broadcasted_iota(jnp.int32, (rows, rows), 0) % 4
        == lax.broadcasted_iota(jnp.int32, (rows, rows), 1) % 4
    )

    def attend(j):
        first = recv[:, 1 + 2 * j].reshape(rows, 128)
        second = recv[:, 2 + 2 * j].reshape(rows, 128)
        rest = recv[:, 0].reshape(rows, 128)
        scores = lax.dot_general(
            first[:, :HD], second[:, :HD], (((1,), (1,)), ((), ())), preferred_element_type=F32
        ) * (1.0 / math.sqrt(HD))
        scores = jnp.where(same, scores, -jnp.inf)
        exponent = jnp.exp(scores - jnp.max(scores, axis=-1, keepdims=True))
        probs = (exponent / jnp.sum(exponent, axis=-1, keepdims=True)).astype(BF16)
        values = jnp.concatenate([first, second, rest], axis=1)
        mixed = jnp.dot(probs, values, preferred_element_type=F32)
        return mixed

    def in_order(first, second, rest, turn):
        return jnp.where(
            lane < 40,
            pltpu.roll(first, 40, 1),
            jnp.where(lane < 80, pltpu.roll(second, 80, 1), pltpu.roll(rest, turn, 1)),
        )

    def straight(mixed, j):
        return in_order(
            mixed[:, 0:128], mixed[:, 128:256], mixed[:, 256:384], (80 - 8 * j) % 128
        )

    def put(n, tile):
        ret_send[:, n] = tile.astype(BF16).reshape(NT, 16, 128)

    to_chip = ((z + xl) % 2) * 4 + (z // 2 + y) % 4

    def ret_copy(to_t, to_core, first, count, sem):
        tiles = pl.ds(first, count)
        to_h = to_chip * 2 + to_core
        own = jnp.logical_and(to_t == t, to_h == h)
        src, dst = ret_send.at[to_t, tiles], ret_recv.at[h, tiles]
        remote = pltpu.make_async_remote_copy(
            src_ref=src, dst_ref=dst, send_sem=rt_send.at[sem, to_t], recv_sem=rt_recv.at[0],
            device_id=(to_t, to_h), device_id_type=MESH,
        )
        return own, remote, lambda: pltpu.make_async_copy(src, dst, rt_recv.at[0])

    def far_first(k):
        n, away = k // 2, (k // 2 + 1) // 2
        off = jnp.where(n % 2 == 0, NZ // 2 - away, NZ // 2 + away)
        return ((xh + 1 - k % 2) % 2) * NZ + (z + off) % NZ

    def ret_first(to_t):
        return ret_copy(to_t, jnp.where(is_a, 0, 1), 0, 2, 0)

    def ret_second_a(to_t):
        return ret_copy(to_t, 0, 2, 2, 1)

    def ret_second_b(to_t):
        return ret_copy(to_t, 1, 2, 1, 1)

    def ret_shared(to_t):
        return ret_copy(to_t, 1, 3, 1, 2)

    p1_wait(0, FIRST)

    mixed2 = attend(2)
    put(0, jnp.where(lane < HD, straight(attend(0), 0), mixed2[:, 0:128]))
    put(1, jnp.where(lane < HD, straight(attend(1), 1), mixed2[:, 128:256]))
    rest2 = pltpu.roll(mixed2[:, 256:384], 72, 1)

    @pl.loop(0, NT)
    def _(k):
        start(ret_first(far_first(k)))

    w_relay(1)

    @pl.when(is_a)
    def _():
        p1_wait(1, SECOND[0])
        put(3, straight(attend(4), 4))

    @pl.when(jnp.logical_not(is_a))
    def _():
        p1_wait(1, SECOND[1])

    put(2, jnp.where(lane < HD, straight(attend(3), 3), rest2))

    @pl.when(is_a)
    def _():
        @pl.loop(0, NT)
        def _(k):
            to_t = far_first(k)
            start(ret_second_a(to_t))
            start(ret_shared(to_t))

    @pl.when(jnp.logical_not(is_a))
    def _():
        @pl.loop(0, NT)
        def _(k):
            start(ret_second_b(far_first(k)))

    w_fourth()
    w_last()

    @pl.loop(0, BLOCKS)
    def _(b):
        for kind in range(2):
            finish(p1_first(b, kind))
            finish(p1_second(b, kind))

    @pl.loop(0, NT)
    def _(to_t):
        finish(ret_first(to_t))

    @pl.when(is_a)
    def _():
        @pl.loop(0, NT)
        def _(to_t):
            finish(ret_second_a(to_t))
            finish(ret_shared(to_t))

    @pl.when(jnp.logical_not(is_a))
    def _():
        @pl.loop(0, NT)
        def _(to_t):
            finish(ret_second_b(to_t))

    for copy in w_sends:
        copy.wait_send()

    pltpu.make_async_copy(ret_recv, ret_recv, rt_recv.at[0]).wait()

    tiles = [ret_recv[:, n] for n in range(RT)]
    parts = [tile.reshape(rows, 128).astype(F32) for tile in tiles[:3]]
    third = in_order(parts[0], parts[1], parts[2], 120).astype(BF16).reshape(NH, 16, 128)
    left = jnp.concatenate(
        [
            jnp.concatenate([quad[g] for g in range(NH)], axis=1)
            for quad in (tiles[0], tiles[1], third, tiles[2], tiles[3])
        ],
        axis=0,
    )
    total = jnp.dot(left, wbuf[...].reshape(NH * 128, D), preferred_element_type=F32)

    for c in range(D // 128):
        rows_out[c] = total[:, 128 * c : 128 * c + 128]
    for o in range(18):
        at = o + 2 * core
        quad = (at // 4 + QA - core) % QA
        for c in range(D // 128):
            out[o, :, pl.ds(128 * c, 128)] = rows_out[
                c, pl.ds(16 * quad + at % 4, FR, stride=4), :
            ].astype(BF16)


def on_device(tokens, norm_gain, norm_shift, w_qkv, output_weight):
    vmem = pl.BlockSpec(memory_space=pltpu.VMEM)
    hbm = pl.BlockSpec(memory_space=pl.ANY)
    dma = pltpu.SemaphoreType.DMA
    rows = pl.pallas_call(
        kernel,
        out_shape=jax.ShapeDtypeStruct((18, FR, D), BF16),
        in_specs=[hbm] * 5,
        out_specs=vmem,
        scratch_shapes=[
            pltpu.VMEM((FR, PATCHES, D), BF16),
            pltpu.VMEM((D,), F32),
            pltpu.VMEM((D,), F32),
            pltpu.VMEM((3 * HD, D), BF16),
            pltpu.VMEM((HD, D), BF16),
            pltpu.VMEM((384, D), BF16),
            pltpu.VMEM((FR, HALF, 384), F32),
            pltpu.VMEM((BLOCKS, 2, TA, 16, 128), BF16),
            pltpu.VMEM((NT, TA, 16, 128), BF16),
            pltpu.VMEM((NT, RT, 16, 128), BF16),
            pltpu.VMEM((NH, RT, 16, 128), BF16),
            pltpu.VMEM((NH, 128, D), BF16),
            pltpu.VMEM((D // 128, 16 * QA, 128), F32),
            dma((2,)),
            dma((4,)),
            dma((2, 2 * BLOCKS)),
            dma((2,)),
            dma((3, NT)),
            dma((1,)),
            dma((18,)),
            dma((18,)),
        ],
        compiler_params=pltpu.CompilerParams(
            collective_id=0, has_side_effects=True, vmem_limit_bytes=55000 * 1024
        ),
        cost_estimate=pl.CostEstimate(
            flops=2 * FR * PATCHES * D * 264 + 2 * 72 * D * D,
            bytes_accessed=5_000_000,
            transcendentals=18 * 64 * 64,
        ),
    )(
        tokens,
        pltpu.with_memory_space_constraint(norm_gain, pltpu.HBM),
        pltpu.with_memory_space_constraint(norm_shift, pltpu.HBM),
        jnp.transpose(w_qkv, (1, 2, 0)).reshape(3 * HD, D),
        output_weight,
    )
    return jnp.transpose(rows, (1, 0, 2))


def solution(mesh):
    return jax.shard_map(
        on_device,
        mesh=mesh,
        in_specs=(P("tm", None, None), P(), P(), P(None, "head", None), P("head", None)),
        out_specs=P("tm", "head", None),
        check_vma=False,
    )
```

```python
import math

import jax
import jax.numpy as jnp
from jax import lax
from jax.experimental import pallas as pl
from jax.experimental.pallas import tpu as pltpu
from jax.sharding import PartitionSpec as P

MESH = pl.DeviceIdType.MESH
D = 1408
HD = 88
FR = 4
PATCHES = 288
NT = 16
NH = 16
NZ = 8
HALF = PATCHES // 2
BLOCKS = 8
QA, QB = 5, 4
TA, TB = 2 * QA + 1, 2 * QB + 1
QFIRST = 3
TFIRST = 2 * QFIRST + 1
RT = 4
WROWS = 96
F32 = jnp.float32
BF16 = jnp.bfloat16


def kernel(
    tok_hbm, gain_hbm, shift_hbm, wq_hbm, wo_hbm, out,
    tok, gain_row, shift_row, wq, wo, wperm, packed, send, recv, ret_send, ret_recv, wbuf, rows_out,
    tok_sem, in_sem, p1_send, p1_recv, rt_send, rt_recv, w_send, w_recv,
):
    t = lax.axis_index("tm")
    h = lax.axis_index("head")
    xh, z = t // NZ, t % NZ
    chip, core = h // 2, h % 2
    y, xl = chip // 2, chip % 2
    is_a = xh == core

    def head_of(y_, xl_, core_):
        return ((y_ + 4) % 4) * 4 + xl_ * 2 + core_

    x_cross = ((1 - xh) * NZ + z, head_of(y, 1 - xl, core))
    barrier = pltpu.get_barrier_semaphore()

    @pl.loop(1, NT)
    def _(k):
        pl.semaphore_signal(barrier, inc=1, device_id=((t + k) % NT, h), device_id_type=MESH)
        pl.semaphore_signal(barrier, inc=1, device_id=(t, (h + k) % NH), device_id_type=MESH)

    pl.semaphore_signal(barrier, inc=1, device_id=x_cross, device_id_type=MESH)

    halves = ((z + xl) % 2, (z + xl + 1) % 2)

    def z_of(block, y_, xl_):
        return ((block % 4 - y_ + 4) % 4) * 2 + (block // 4 + xl_) % 2

    def half_rows(n):
        return pl.ds(pl.multiple_of(halves[n] * HALF, 16), HALF)

    tok_copies = [
        pltpu.make_async_copy(
            tok_hbm.at[:, half_rows(n), :], tok.at[:, half_rows(n), :], tok_sem.at[n]
        )
        for n in range(2)
    ]
    wq_copy = pltpu.make_async_copy(wq_hbm, wq, in_sem.at[0])
    wo_copy = pltpu.make_async_copy(wo_hbm, wo, in_sem.at[1])
    gain_copy = pltpu.make_async_copy(gain_hbm, gain_row, in_sem.at[2])
    shift_copy = pltpu.make_async_copy(shift_hbm, shift_row, in_sem.at[3])
    tok_copies[0].start()
    wq_copy.start()
    wo_copy.start()
    gain_copy.start()
    shift_copy.start()
    tok_copies[1].start()

    wq_copy.wait()
    w = wq[...].astype(F32)
    wperm[...] = jnp.concatenate(
        [w[0:88], w[176:216], w[88:176], w[216:264], jnp.zeros((120, D), F32)], axis=0
    ).astype(BF16)
    gain_copy.wait()
    shift_copy.wait()
    gain = gain_row[...].reshape(1, D)
    shift = shift_row[...].reshape(1, D)

    def project(n):
        tok_copies[n].wait()
        values = tok[:, half_rows(n), :].reshape(FR * HALF, D).astype(F32)
        average = jnp.mean(values, axis=-1, keepdims=True)
        centred = values - average
        var = jnp.mean(centred * centred, axis=-1, keepdims=True)
        normed = centred * lax.rsqrt(var + 1e-06) * gain + shift
        normed = normed.astype(BF16)

        packed[...] = lax.dot_general(
            normed, wperm[...],
            (((1,), (1,)), ((), ())), preferred_element_type=F32,
        ).reshape(FR, HALF, 384)

        parts = [packed[f].reshape(HALF // 8, 8, 384) for f in range(FR)]
        low = lax.broadcasted_iota(jnp.int32, parts[0].shape, 1) < 4
        turned = [pltpu.roll(part, 4, 1) for part in parts]
        even = jnp.concatenate(
            [jnp.where(low, parts[0], turned[1]), jnp.where(low, parts[2], turned[3])], axis=1
        )
        odd = jnp.concatenate(
            [jnp.where(low, turned[0], parts[1]), jnp.where(low, turned[2], parts[3])], axis=1
        )
        for b in range(BLOCKS // 2):
            for kind, first, count in ((0, 0, QA), (1, QA, QB)):
                rest = None
                for j in range(count):
                    q = 9 * b + first + j
                    tile = (odd if q % 2 else even)[q // 2]
                    at = halves[n] * (BLOCKS // 2) + b
                    send[at, kind, 1 + 2 * j] = tile[:, 0:128].astype(BF16)
                    send[at, kind, 2 + 2 * j] = tile[:, 128:256].astype(BF16)
                    left = tile[:, 256:384]
                    if j:
                        left = pltpu.roll(left, 8 * j, 1)
                    rest = left if rest is None else rest + left
                send[at, kind, 0] = rest.astype(BF16)

    def p1_to(b, kind):
        return jnp.where(kind == 0, core, 1 - core) * NZ + z_of(b, y, xl)

    def p1_copy(b, kind, group, tiles):
        src, dst = send.at[b, kind, tiles], recv.at[t, tiles]
        to_t = p1_to(b, kind)
        remote = pltpu.make_async_remote_copy(
            src_ref=src, dst_ref=dst, send_sem=p1_send.at[group, 2 * b + kind],
            recv_sem=p1_recv.at[group], device_id=(to_t, h), device_id_type=MESH,
        )
        return to_t == t, remote, lambda: pltpu.make_async_copy(src, dst, p1_recv.at[group])

    def start(triple):
        own, remote, local = triple

        @pl.when(own)
        def _():
            local().start()

        @pl.when(jnp.logical_not(own))
        def _():
            remote.start()

    def finish(triple):
        own, remote, _ = triple

        @pl.when(jnp.logical_not(own))
        def _():
            remote.wait_send()

    def p1_first(b, kind):
        return p1_copy(b, kind, 0, FIRST)

    def p1_second(b, kind):
        return p1_copy(b, kind, 1, SECOND[kind])

    FIRST = pl.ds(0, TFIRST)
    SECOND = (pl.ds(TFIRST, TA - TFIRST), pl.ds(TFIRST, TB - TFIRST))

    def block_at(n, step):
        off = step + 2 if n == 0 else step + 1 + z % 2
        return halves[n] * (BLOCKS // 2) + (z // 2 + off + y) % (BLOCKS // 2)

    def start_first(n):
        @pl.loop(0, BLOCKS // 2)
        def _(step):
            b = block_at(n, step)
            start(p1_first(b, jnp.where(is_a, 1, 0)))
            start(p1_first(b, jnp.where(is_a, 0, 1)))

    def start_second(n):
        @pl.loop(0, BLOCKS // 2)
        def _(step):
            b = block_at(n, step)
            start(p1_second(b, 0))
            start(p1_second(b, 1))

    sib = (t, chip * 2 + 1 - core)
    x_near = (t, head_of(y, 1 - xl, core))
    y_up, y_down = (t, head_of(y + 1, xl, core)), (t, head_of(y - 1, xl, core))
    slot_x = head_of(y, 1 - xl, core)
    FULL, LOW, HIGH = (0, WROWS), (0, WROWS // 2), (WROWS // 2, WROWS // 2)

    def w_copy(slot, rows, to, n_send, n_recv):
        ref = wbuf.at[slot, pl.ds(rows[0], rows[1]), :]
        return pltpu.make_async_remote_copy(
            src_ref=ref, dst_ref=ref, send_sem=w_send.at[n_send], recv_sem=w_recv.at[n_recv],
            device_id=to, device_id_type=MESH,
        )

    def slot(dy, other_x, other_core):
        return head_of(y + dy, (1 - xl) if other_x else xl, (1 - core) if other_core else core)

    w_sends = []

    def w_start(copy):
        copy.start()
        w_sends.append(copy)

    def w_wait(slot_, rows, n_recv):
        w_copy(slot_, rows, sib, 0, n_recv).wait_recv()

    def w_first():
        w_start(w_copy(h, LOW, x_near, 0, 8))
        w_start(w_copy(h, HIGH, x_cross, 1, 9))
        w_start(w_copy(h, FULL, y_up, 2, 10))
        w_start(w_copy(h, FULL, y_down, 3, 11))
        w_start(w_copy(h, FULL, sib, 4, 0))

    def w_second():
        w_wait(slot_x, LOW, 8)
        w_wait(slot_x, HIGH, 9)
        w_start(w_copy(slot_x, FULL, y_up, 5, 12))
        w_start(w_copy(slot_x, FULL, y_down, 6, 13))
        w_start(w_copy(slot_x, FULL, sib, 7, 1))

    def w_relay(other_x):
        for n, (dy, rows, to) in enumerate(((-1, LOW, y_up), (1, HIGH, y_down))):
            n += 2 * other_x
            at = slot(dy, other_x, 0)
            w_wait(at, FULL, 10 + n)
            w_start(w_copy(at, rows, to, 8 + n, 14 + n))
            w_start(w_copy(at, FULL, sib, 12 + n, 2 + n))

    def w_fourth():
        for other_x in (0, 1):
            at = slot(2, other_x, 0)
            w_wait(at, LOW, 14 + 2 * other_x)
            w_wait(at, HIGH, 15 + 2 * other_x)
            w_start(w_copy(at, FULL, sib, 16 + other_x, 6 + other_x))

    def w_last():
        for n, (dy, other_x) in enumerate(
            ((0, 0), (0, 1), (-1, 0), (1, 0), (-1, 1), (1, 1), (2, 0), (2, 1))
        ):
            w_wait(slot(dy, other_x, 1), FULL, n)

    wo_copy.wait()
    wbuf[h, pl.ds(0, WROWS), :] = jnp.concatenate(
        [wo[...].astype(F32), jnp.zeros((WROWS - HD, D), F32)], axis=0
    ).astype(BF16)

    @pl.loop(0, NH)
    def _(k):
        wbuf[k, pl.ds(WROWS, 128 - WROWS), :] = jnp.zeros((128 - WROWS, D), BF16)

    project(0)
    pl.semaphore_wait(barrier, 2 * (NT - 1) + 1)
    w_first()
    start_first(0)
    project(1)
    start_first(1)
    start_second(0)
    start_second(1)
    w_second()
    w_relay(0)

    def p1_wait(group, tiles):
        ref = recv.at[:, tiles]
        pltpu.make_async_copy(ref, ref, p1_recv.at[group]).wait()

    rows = 16 * NT
    lane = lax.broadcasted_iota(jnp.int32, (rows, 128), 1)
    same = (
        lax.broadcasted_iota(jnp.int32, (rows, rows), 0) % 4
        == lax.broadcasted_iota(jnp.int32, (rows, rows), 1) % 4
    )

    def attend(j):
        first = recv[:, 1 + 2 * j].reshape(rows, 128)
        second = recv[:, 2 + 2 * j].reshape(rows, 128)
        rest = recv[:, 0].reshape(rows, 128)
        scores = lax.dot_general(
            first[:, :HD], second[:, :HD], (((1,), (1,)), ((), ())), preferred_element_type=F32
        ) * (1.0 / math.sqrt(HD))
        scores = jnp.where(same, scores, -jnp.inf)
        exponent = jnp.exp(scores - jnp.max(scores, axis=-1, keepdims=True))
        probs = (exponent / jnp.sum(exponent, axis=-1, keepdims=True)).astype(BF16)
        values = jnp.concatenate([first, second, rest], axis=1)
        mixed = jnp.dot(probs, values, preferred_element_type=F32)
        return mixed

    def in_order(first, second, rest, turn):
        return jnp.where(
            lane < 40,
            pltpu.roll(first, 40, 1),
            jnp.where(lane < 80, pltpu.roll(second, 80, 1), pltpu.roll(rest, turn, 1)),
        )

    def straight(mixed, j):
        return in_order(
            mixed[:, 0:128], mixed[:, 128:256], mixed[:, 256:384], (80 - 8 * j) % 128
        )

    def put(n, tile):
        ret_send[:, n] = tile.astype(BF16).reshape(NT, 16, 128)

    to_chip = ((z + xl) % 2) * 4 + (z // 2 + y) % 4

    def ret_copy(to_t, to_core, first, count, sem):
        tiles = pl.ds(first, count)
        to_h = to_chip * 2 + to_core
        own = jnp.logical_and(to_t == t, to_h == h)
        src, dst = ret_send.at[to_t, tiles], ret_recv.at[h, tiles]
        remote = pltpu.make_async_remote_copy(
            src_ref=src, dst_ref=dst, send_sem=rt_send.at[sem, to_t], recv_sem=rt_recv.at[0],
            device_id=(to_t, to_h), device_id_type=MESH,
        )
        return own, remote, lambda: pltpu.make_async_copy(src, dst, rt_recv.at[0])

    def far_first(k):
        n, away = k // 2, (k // 2 + 1) // 2
        off = jnp.where(n % 2 == 0, NZ // 2 - away, NZ // 2 + away)
        return ((xh + 1 - k % 2) % 2) * NZ + (z + off) % NZ

    def ret_first(to_t):
        return ret_copy(to_t, jnp.where(is_a, 0, 1), 0, 2, 0)

    def ret_second_a(to_t):
        return ret_copy(to_t, 0, 2, 2, 1)

    def ret_second_b(to_t):
        return ret_copy(to_t, 1, 2, 1, 1)

    def ret_shared(to_t):
        return ret_copy(to_t, 1, 3, 1, 2)

    p1_wait(0, FIRST)

    mixed2 = attend(2)
    put(0, jnp.where(lane < HD, straight(attend(0), 0), mixed2[:, 0:128]))
    put(1, jnp.where(lane < HD, straight(attend(1), 1), mixed2[:, 128:256]))
    rest2 = pltpu.roll(mixed2[:, 256:384], 72, 1)

    @pl.loop(0, NT)
    def _(k):
        start(ret_first(far_first(k)))

    w_relay(1)

    @pl.when(is_a)
    def _():
        p1_wait(1, SECOND[0])
        put(3, straight(attend(4), 4))

    @pl.when(jnp.logical_not(is_a))
    def _():
        p1_wait(1, SECOND[1])

    put(2, jnp.where(lane < HD, straight(attend(3), 3), rest2))

    @pl.when(is_a)
    def _():
        @pl.loop(0, NT)
        def _(k):
            to_t = far_first(k)
            start(ret_second_a(to_t))
            start(ret_shared(to_t))

    @pl.when(jnp.logical_not(is_a))
    def _():
        @pl.loop(0, NT)
        def _(k):
            start(ret_second_b(far_first(k)))

    w_fourth()
    w_last()

    @pl.loop(0, BLOCKS)
    def _(b):
        for kind in range(2):
            finish(p1_first(b, kind))
            finish(p1_second(b, kind))

    @pl.loop(0, NT)
    def _(to_t):
        finish(ret_first(to_t))

    @pl.when(is_a)
    def _():
        @pl.loop(0, NT)
        def _(to_t):
            finish(ret_second_a(to_t))
            finish(ret_shared(to_t))

    @pl.when(jnp.logical_not(is_a))
    def _():
        @pl.loop(0, NT)
        def _(to_t):
            finish(ret_second_b(to_t))

    for copy in w_sends:
        copy.wait_send()

    pltpu.make_async_copy(ret_recv, ret_recv, rt_recv.at[0]).wait()

    tiles = [ret_recv[:, n] for n in range(RT)]
    parts = [tile.reshape(rows, 128).astype(F32) for tile in tiles[:3]]
    third = in_order(parts[0], parts[1], parts[2], 120).astype(BF16).reshape(NH, 16, 128)
    left = jnp.concatenate(
        [
            jnp.concatenate([quad[g] for g in range(NH)], axis=1)
            for quad in (tiles[0], tiles[1], third, tiles[2], tiles[3])
        ],
        axis=0,
    )
    total = jnp.dot(left, wbuf[...].reshape(NH * 128, D), preferred_element_type=F32)

    for c in range(D // 128):
        rows_out[c] = total[:, 128 * c : 128 * c + 128]
    for o in range(18):
        at = o + 2 * core
        quad = (at // 4 + QA - core) % QA
        for c in range(D // 128):
            out[o, :, pl.ds(128 * c, 128)] = rows_out[
                c, pl.ds(16 * quad + at % 4, FR, stride=4), :
            ].astype(BF16)


def on_device(tokens, norm_gain, norm_shift, w_qkv, output_weight):
    vmem = pl.BlockSpec(memory_space=pltpu.VMEM)
    hbm = pl.BlockSpec(memory_space=pl.ANY)
    dma = pltpu.SemaphoreType.DMA
    rows = pl.pallas_call(
        kernel,
        out_shape=jax.ShapeDtypeStruct((18, FR, D), BF16),
        in_specs=[hbm] * 5,
        out_specs=vmem,
        scratch_shapes=[
            pltpu.VMEM((FR, PATCHES, D), BF16),
            pltpu.VMEM((D,), F32),
            pltpu.VMEM((D,), F32),
            pltpu.VMEM((3 * HD, D), BF16),
            pltpu.VMEM((HD, D), BF16),
            pltpu.VMEM((384, D), BF16),
            pltpu.VMEM((FR, HALF, 384), F32),
            pltpu.VMEM((BLOCKS, 2, TA, 16, 128), BF16),
            pltpu.VMEM((NT, TA, 16, 128), BF16),
            pltpu.VMEM((NT, RT, 16, 128), BF16),
            pltpu.VMEM((NH, RT, 16, 128), BF16),
            pltpu.VMEM((NH, 128, D), BF16),
            pltpu.VMEM((D // 128, 16 * QA, 128), F32),
            dma((2,)),
            dma((4,)),
            dma((2, 2 * BLOCKS)),
            dma((2,)),
            dma((3, NT)),
            dma((1,)),
            dma((18,)),
            dma((18,)),
        ],
        compiler_params=pltpu.CompilerParams(
            collective_id=0, has_side_effects=True, vmem_limit_bytes=55000 * 1024
        ),
        cost_estimate=pl.CostEstimate(
            flops=2 * FR * PATCHES * D * 264 + 2 * 72 * D * D,
            bytes_accessed=5_000_000,
            transcendentals=18 * 64 * 64,
        ),
    )(
        tokens,
        pltpu.with_memory_space_constraint(norm_gain, pltpu.HBM),
        pltpu.with_memory_space_constraint(norm_shift, pltpu.HBM),
        jnp.transpose(w_qkv, (1, 2, 0)).reshape(3 * HD, D),
        output_weight,
    )
    return jnp.transpose(rows, (1, 0, 2))


def solution(mesh):
    return jax.shard_map(
        on_device,
        mesh=mesh,
        in_specs=(P("tm", None, None), P(), P(), P(None, "head", None), P("head", None)),
        out_specs=P("tm", "head", None),
        check_vma=False,
    )
```

```python
import math

import jax
import jax.numpy as jnp
from jax import lax
from jax.experimental import pallas as pl
from jax.experimental.pallas import tpu as pltpu
from jax.sharding import PartitionSpec as P

MESH = pl.DeviceIdType.MESH
D = 1408
HD = 88
FR = 4
PATCHES = 288
NT = 16
NH = 16
NZ = 8
HALF = PATCHES // 2
BLOCKS = 8
QA, QB = 5, 4
TA, TB = 2 * QA + 1, 2 * QB + 1
QFIRST = 3
TFIRST = 2 * QFIRST + 1
RT = 4
WROWS = 96
F32 = jnp.float32
BF16 = jnp.bfloat16


def kernel(
    tok_hbm, gain_hbm, shift_hbm, wq_hbm, wo_hbm, out,
    tok, gain_row, shift_row, wq, wo, wperm, packed, send, recv, ret_send, ret_recv, wbuf, rows_out,
    tok_sem, in_sem, p1_send, p1_recv, rt_send, rt_recv, w_send, w_recv,
):
    t = lax.axis_index("tm")
    h = lax.axis_index("head")
    xh, z = t // NZ, t % NZ
    chip, core = h // 2, h % 2
    y, xl = chip // 2, chip % 2
    is_a = xh == core

    def head_of(y_, xl_, core_):
        return ((y_ + 4) % 4) * 4 + xl_ * 2 + core_

    x_cross = ((1 - xh) * NZ + z, head_of(y, 1 - xl, core))
    barrier = pltpu.get_barrier_semaphore()

    @pl.loop(1, NT)
    def _(k):
        pl.semaphore_signal(barrier, inc=1, device_id=((t + k) % NT, h), device_id_type=MESH)
        pl.semaphore_signal(barrier, inc=1, device_id=(t, (h + k) % NH), device_id_type=MESH)

    pl.semaphore_signal(barrier, inc=1, device_id=x_cross, device_id_type=MESH)

    halves = ((z + xl) % 2, (z + xl + 1) % 2)

    def z_of(block, y_, xl_):
        return ((block % 4 - y_ + 4) % 4) * 2 + (block // 4 + xl_) % 2

    def half_rows(n):
        return pl.ds(pl.multiple_of(halves[n] * HALF, 16), HALF)

    tok_copies = [
        pltpu.make_async_copy(
            tok_hbm.at[:, half_rows(n), :], tok.at[:, half_rows(n), :], tok_sem.at[n]
        )
        for n in range(2)
    ]
    wq_copy = pltpu.make_async_copy(wq_hbm, wq, in_sem.at[0])
    wo_copy = pltpu.make_async_copy(wo_hbm, wo, in_sem.at[1])
    gain_copy = pltpu.make_async_copy(gain_hbm, gain_row, in_sem.at[2])
    shift_copy = pltpu.make_async_copy(shift_hbm, shift_row, in_sem.at[3])
    tok_copies[0].start()
    wq_copy.start()
    wo_copy.start()
    gain_copy.start()
    shift_copy.start()
    tok_copies[1].start()

    wq_copy.wait()
    w = wq[...].astype(F32)
    wperm[...] = jnp.concatenate(
        [w[0:88], w[176:216], w[88:176], w[216:264], jnp.zeros((120, D), F32)], axis=0
    ).astype(BF16)
    gain_copy.wait()
    shift_copy.wait()
    gain = gain_row[...].reshape(1, D)
    shift = shift_row[...].reshape(1, D)

    def project(n):
        tok_copies[n].wait()
        values = tok[:, half_rows(n), :].reshape(FR * HALF, D).astype(F32)
        average = jnp.mean(values, axis=-1, keepdims=True)
        centred = values - average
        var = jnp.mean(centred * centred, axis=-1, keepdims=True)
        normed = centred * lax.rsqrt(var + 1e-06) * gain + shift
        normed = normed.astype(BF16)

        packed[...] = lax.dot_general(
            normed, wperm[...],
            (((1,), (1,)), ((), ())), preferred_element_type=F32,
        ).reshape(FR, HALF, 384)

        parts = [packed[f].reshape(HALF // 8, 8, 384) for f in range(FR)]
        low = lax.broadcasted_iota(jnp.int32, parts[0].shape, 1) < 4
        turned = [pltpu.roll(part, 4, 1) for part in parts]
        even = jnp.concatenate(
            [jnp.where(low, parts[0], turned[1]), jnp.where(low, parts[2], turned[3])], axis=1
        )
        odd = jnp.concatenate(
            [jnp.where(low, turned[0], parts[1]), jnp.where(low, turned[2], parts[3])], axis=1
        )
        for b in range(BLOCKS // 2):
            for kind, first, count in ((0, 0, QA), (1, QA, QB)):
                rest = None
                for j in range(count):
                    q = 9 * b + first + j
                    tile = (odd if q % 2 else even)[q // 2]
                    at = halves[n] * (BLOCKS // 2) + b
                    send[at, kind, 1 + 2 * j] = tile[:, 0:128].astype(BF16)
                    send[at, kind, 2 + 2 * j] = tile[:, 128:256].astype(BF16)
                    left = tile[:, 256:384]
                    if j:
                        left = pltpu.roll(left, 8 * j, 1)
                    rest = left if rest is None else rest + left
                send[at, kind, 0] = rest.astype(BF16)

    def p1_to(b, kind):
        return jnp.where(kind == 0, core, 1 - core) * NZ + z_of(b, y, xl)

    def p1_copy(b, kind, group, tiles):
        src, dst = send.at[b, kind, tiles], recv.at[t, tiles]
        to_t = p1_to(b, kind)
        remote = pltpu.make_async_remote_copy(
            src_ref=src, dst_ref=dst, send_sem=p1_send.at[group, 2 * b + kind],
            recv_sem=p1_recv.at[group], device_id=(to_t, h), device_id_type=MESH,
        )
        return to_t == t, remote, lambda: pltpu.make_async_copy(src, dst, p1_recv.at[group])

    def start(triple):
        own, remote, local = triple

        @pl.when(own)
        def _():
            local().start()

        @pl.when(jnp.logical_not(own))
        def _():
            remote.start()

    def finish(triple):
        own, remote, _ = triple

        @pl.when(jnp.logical_not(own))
        def _():
            remote.wait_send()

    def p1_first(b, kind):
        return p1_copy(b, kind, 0, FIRST)

    def p1_second(b, kind):
        return p1_copy(b, kind, 1, SECOND[kind])

    FIRST = pl.ds(0, TFIRST)
    SECOND = (pl.ds(TFIRST, TA - TFIRST), pl.ds(TFIRST, TB - TFIRST))

    def block_at(n, step):
        off = step + 2 if n == 0 else step + 1 + z % 2
        return halves[n] * (BLOCKS // 2) + (z // 2 + off + y) % (BLOCKS // 2)

    def start_first(n):
        @pl.loop(0, BLOCKS // 2)
        def _(step):
            b = block_at(n, step)
            start(p1_first(b, jnp.where(is_a, 1, 0)))
            start(p1_first(b, jnp.where(is_a, 0, 1)))

    def start_second(n):
        @pl.loop(0, BLOCKS // 2)
        def _(step):
            b = block_at(n, step)
            start(p1_second(b, 0))
            start(p1_second(b, 1))

    sib = (t, chip * 2 + 1 - core)
    x_near = (t, head_of(y, 1 - xl, core))
    y_up, y_down = (t, head_of(y + 1, xl, core)), (t, head_of(y - 1, xl, core))
    slot_x = head_of(y, 1 - xl, core)
    FULL, LOW, HIGH = (0, WROWS), (0, WROWS // 2), (WROWS // 2, WROWS // 2)

    def w_copy(slot, rows, to, n_send, n_recv):
        ref = wbuf.at[slot, pl.ds(rows[0], rows[1]), :]
        return pltpu.make_async_remote_copy(
            src_ref=ref, dst_ref=ref, send_sem=w_send.at[n_send], recv_sem=w_recv.at[n_recv],
            device_id=to, device_id_type=MESH,
        )

    def slot(dy, other_x, other_core):
        return head_of(y + dy, (1 - xl) if other_x else xl, (1 - core) if other_core else core)

    w_sends = []

    def w_start(copy):
        copy.start()
        w_sends.append(copy)

    def w_wait(slot_, rows, n_recv):
        w_copy(slot_, rows, sib, 0, n_recv).wait_recv()

    def w_first():
        w_start(w_copy(h, LOW, x_near, 0, 8))
        w_start(w_copy(h, HIGH, x_cross, 1, 9))
        w_start(w_copy(h, FULL, y_up, 2, 10))
        w_start(w_copy(h, FULL, y_down, 3, 11))
        w_start(w_copy(h, FULL, sib, 4, 0))

    def w_second():
        w_wait(slot_x, LOW, 8)
        w_wait(slot_x, HIGH, 9)
        w_start(w_copy(slot_x, FULL, y_up, 5, 12))
        w_start(w_copy(slot_x, FULL, y_down, 6, 13))
        w_start(w_copy(slot_x, FULL, sib, 7, 1))

    def w_relay(other_x):
        for n, (dy, rows, to) in enumerate(((-1, LOW, y_up), (1, HIGH, y_down))):
            n += 2 * other_x
            at = slot(dy, other_x, 0)
            w_wait(at, FULL, 10 + n)
            w_start(w_copy(at, rows, to, 8 + n, 14 + n))
            w_start(w_copy(at, FULL, sib, 12 + n, 2 + n))

    def w_fourth():
        for other_x in (0, 1):
            at = slot(2, other_x, 0)
            w_wait(at, LOW, 14 + 2 * other_x)
            w_wait(at, HIGH, 15 + 2 * other_x)
            w_start(w_copy(at, FULL, sib, 16 + other_x, 6 + other_x))

    def w_last():
        for n, (dy, other_x) in enumerate(
            ((0, 0), (0, 1), (-1, 0), (1, 0), (-1, 1), (1, 1), (2, 0), (2, 1))
        ):
            w_wait(slot(dy, other_x, 1), FULL, n)

    wo_copy.wait()
    wbuf[h, pl.ds(0, WROWS), :] = jnp.concatenate(
        [wo[...].astype(F32), jnp.zeros((WROWS - HD, D), F32)], axis=0
    ).astype(BF16)

    @pl.loop(0, NH)
    def _(k):
        wbuf[k, pl.ds(WROWS, 128 - WROWS), :] = jnp.zeros((128 - WROWS, D), BF16)

    project(0)
    pl.semaphore_wait(barrier, 2 * (NT - 1) + 1)
    w_first()
    start_first(0)
    project(1)
    start_first(1)
    start_second(0)
    start_second(1)
    w_second()
    w_relay(0)

    def p1_wait(group, tiles):
        ref = recv.at[:, tiles]
        pltpu.make_async_copy(ref, ref, p1_recv.at[group]).wait()

    rows = 16 * NT
    lane = lax.broadcasted_iota(jnp.int32, (rows, 128), 1)
    same = (
        lax.broadcasted_iota(jnp.int32, (rows, rows), 0) % 4
        == lax.broadcasted_iota(jnp.int32, (rows, rows), 1) % 4
    )

    def attend(j):
        first = recv[:, 1 + 2 * j].reshape(rows, 128)
        second = recv[:, 2 + 2 * j].reshape(rows, 128)
        rest = recv[:, 0].reshape(rows, 128)
        scores = lax.dot_general(
            first[:, :HD], second[:, :HD], (((1,), (1,)), ((), ())), preferred_element_type=F32
        ) * (1.0 / math.sqrt(HD))
        scores = jnp.where(same, scores, -jnp.inf)
        exponent = jnp.exp(scores - jnp.max(scores, axis=-1, keepdims=True))
        probs = (exponent / jnp.sum(exponent, axis=-1, keepdims=True)).astype(BF16)
        values = jnp.concatenate([first, second, rest], axis=1)
        mixed = jnp.dot(probs, values, preferred_element_type=F32)
        return mixed

    def in_order(first, second, rest, turn):
        return jnp.where(
            lane < 40,
            pltpu.roll(first, 40, 1),
            jnp.where(lane < 80, pltpu.roll(second, 80, 1), pltpu.roll(rest, turn, 1)),
        )

    def straight(mixed, j):
        return in_order(
            mixed[:, 0:128], mixed[:, 128:256], mixed[:, 256:384], (80 - 8 * j) % 128
        )

    def put(n, tile):
        ret_send[:, n] = tile.astype(BF16).reshape(NT, 16, 128)

    to_chip = ((z + xl) % 2) * 4 + (z // 2 + y) % 4

    def ret_copy(to_t, to_core, first, count, sem):
        tiles = pl.ds(first, count)
        to_h = to_chip * 2 + to_core
        own = jnp.logical_and(to_t == t, to_h == h)
        src, dst = ret_send.at[to_t, tiles], ret_recv.at[h, tiles]
        remote = pltpu.make_async_remote_copy(
            src_ref=src, dst_ref=dst, send_sem=rt_send.at[sem, to_t], recv_sem=rt_recv.at[0],
            device_id=(to_t, to_h), device_id_type=MESH,
        )
        return own, remote, lambda: pltpu.make_async_copy(src, dst, rt_recv.at[0])

    def far_first(k):
        n, away = k // 2, (k // 2 + 1) // 2
        off = jnp.where(n % 2 == 0, NZ // 2 - away, NZ // 2 + away)
        return ((xh + 1 - k % 2) % 2) * NZ + (z + off) % NZ

    def ret_first(to_t):
        return ret_copy(to_t, jnp.where(is_a, 0, 1), 0, 2, 0)

    def ret_second_a(to_t):
        return ret_copy(to_t, 0, 2, 2, 1)

    def ret_second_b(to_t):
        return ret_copy(to_t, 1, 2, 1, 1)

    def ret_shared(to_t):
        return ret_copy(to_t, 1, 3, 1, 2)

    p1_wait(0, FIRST)

    mixed2 = attend(2)
    put(0, jnp.where(lane < HD, straight(attend(0), 0), mixed2[:, 0:128]))
    put(1, jnp.where(lane < HD, straight(attend(1), 1), mixed2[:, 128:256]))
    rest2 = pltpu.roll(mixed2[:, 256:384], 72, 1)

    @pl.loop(0, NT)
    def _(k):
        start(ret_first(far_first(k)))

    w_relay(1)

    @pl.when(is_a)
    def _():
        p1_wait(1, SECOND[0])
        mixed3, mixed4 = attend(3), attend(4)
        put(2, jnp.where(lane < HD, straight(mixed3, 3), rest2))
        put(3, straight(mixed4, 4))

        @pl.loop(0, NT)
        def _(k):
            to_t = far_first(k)
            start(ret_second_a(to_t))
            start(ret_shared(to_t))

    @pl.when(jnp.logical_not(is_a))
    def _():
        p1_wait(1, SECOND[1])
        put(2, jnp.where(lane < HD, straight(attend(3), 3), rest2))

        @pl.loop(0, NT)
        def _(k):
            start(ret_second_b(far_first(k)))

    w_fourth()
    w_last()

    @pl.loop(0, BLOCKS)
    def _(b):
        for kind in range(2):
            finish(p1_first(b, kind))
            finish(p1_second(b, kind))

    @pl.loop(0, NT)
    def _(to_t):
        finish(ret_first(to_t))

    @pl.when(is_a)
    def _():
        @pl.loop(0, NT)
        def _(to_t):
            finish(ret_second_a(to_t))
            finish(ret_shared(to_t))

    @pl.when(jnp.logical_not(is_a))
    def _():
        @pl.loop(0, NT)
        def _(to_t):
            finish(ret_second_b(to_t))

    for copy in w_sends:
        copy.wait_send()

    pltpu.make_async_copy(ret_recv, ret_recv, rt_recv.at[0]).wait()

    tiles = [ret_recv[:, n] for n in range(RT)]
    parts = [tile.reshape(rows, 128).astype(F32) for tile in tiles[:3]]
    third = in_order(parts[0], parts[1], parts[2], 120).astype(BF16).reshape(NH, 16, 128)
    left = jnp.concatenate(
        [
            jnp.concatenate([quad[g] for g in range(NH)], axis=1)
            for quad in (tiles[0], tiles[1], third, tiles[2], tiles[3])
        ],
        axis=0,
    )
    total = jnp.dot(left, wbuf[...].reshape(NH * 128, D), preferred_element_type=F32)

    for c in range(D // 128):
        rows_out[c] = total[:, 128 * c : 128 * c + 128]
    for o in range(18):
        at = o + 2 * core
        quad = (at // 4 + QA - core) % QA
        for c in range(D // 128):
            out[o, :, pl.ds(128 * c, 128)] = rows_out[
                c, pl.ds(16 * quad + at % 4, FR, stride=4), :
            ].astype(BF16)


def on_device(tokens, norm_gain, norm_shift, w_qkv, output_weight):
    vmem = pl.BlockSpec(memory_space=pltpu.VMEM)
    hbm = pl.BlockSpec(memory_space=pl.ANY)
    dma = pltpu.SemaphoreType.DMA
    rows = pl.pallas_call(
        kernel,
        out_shape=jax.ShapeDtypeStruct((18, FR, D), BF16),
        in_specs=[hbm] * 5,
        out_specs=vmem,
        scratch_shapes=[
            pltpu.VMEM((FR, PATCHES, D), BF16),
            pltpu.VMEM((D,), F32),
            pltpu.VMEM((D,), F32),
            pltpu.VMEM((3 * HD, D), BF16),
            pltpu.VMEM((HD, D), BF16),
            pltpu.VMEM((384, D), BF16),
            pltpu.VMEM((FR, HALF, 384), F32),
            pltpu.VMEM((BLOCKS, 2, TA, 16, 128), BF16),
            pltpu.VMEM((NT, TA, 16, 128), BF16),
            pltpu.VMEM((NT, RT, 16, 128), BF16),
            pltpu.VMEM((NH, RT, 16, 128), BF16),
            pltpu.VMEM((NH, 128, D), BF16),
            pltpu.VMEM((D // 128, 16 * QA, 128), F32),
            dma((2,)),
            dma((4,)),
            dma((2, 2 * BLOCKS)),
            dma((2,)),
            dma((3, NT)),
            dma((1,)),
            dma((18,)),
            dma((18,)),
        ],
        compiler_params=pltpu.CompilerParams(
            collective_id=0, has_side_effects=True, vmem_limit_bytes=55000 * 1024
        ),
        cost_estimate=pl.CostEstimate(
            flops=2 * FR * PATCHES * D * 264 + 2 * 72 * D * D,
            bytes_accessed=5_000_000,
            transcendentals=18 * 64 * 64,
        ),
    )(
        tokens,
        pltpu.with_memory_space_constraint(norm_gain, pltpu.HBM),
        pltpu.with_memory_space_constraint(norm_shift, pltpu.HBM),
        jnp.transpose(w_qkv, (1, 2, 0)).reshape(3 * HD, D),
        output_weight,
    )
    return jnp.transpose(rows, (1, 0, 2))


def solution(mesh):
    return jax.shard_map(
        on_device,
        mesh=mesh,
        in_specs=(P("tm", None, None), P(), P(), P(None, "head", None), P("head", None)),
        out_specs=P("tm", "head", None),
        check_vma=False,
    )
```
